256 devices in a mesh: seq: 16 (over y_lo, x, core), grp: 16 (over z, y_hi).
Axes of the slice: x: 4, y: 4 (y_hi: 2, y_lo: 2; y = y_hi * 2 + y_lo), z: 8, core: 2. Of those that a mesh axis runs over, the one named last changes fastest.
Arguments:
- query_in: bfloat16 [32768, 8192], P('seq', 'grp'), may hold values from -6 to 6
- key_in: bfloat16 [32768, 8192], P('seq', 'grp'), may hold values from -6 to 6
- value_in: bfloat16 [32768, 8192], P('seq', 'grp'), may hold values from -6 to 6
- gate_in: bfloat16 [32768, 8192], P('seq', 'grp'), may hold values from -6 to 6
- norm_gain: float32 [8192], P('grp'), may hold values from 0.1 to 1.9
- head_owner: int32 [16], replicated, may hold values from 0 to 15, each once
Outputs:
- attn_out: bfloat16 [32768, 8192], P('seq', 'grp')
- decode_state: float32 [64, 128, 128], P('grp', 'seq')
The draws below stay inside these ranges and needn't reach their ends.
Inputs may be any that keep to these rules, and one draw needn't show every extreme that they name: head_owner is a permutation of the head groups.
All inputs are finite; a program needn't handle non-finite values.
Results may differ from the reference program's by a relative error of at most 0.0095.
Values sent between devices are 32-bit elements; how exact they have to be, the bound alone decides.
No kernel may reach another device: no remote copies, remote signals or barrier semaphores. Data moves between devices by JAX's collectives and lax.ppermute only.
A program may use at most 128 MiB of HBM per device.

```python
import math
import jax
import jax.numpy as jnp
from jax import lax

DH = 128
HEADS_DEV = 4
HEADS = 64
TOKENS = 32768
N_GRP = 16


def draw_value_in(key, part):
    key = jax.random.fold_in(key, 7)
    shape = (TOKENS, HEADS * DH)
    values = jax.random.truncated_normal(key, -5.5, 6.5, shape, jnp.float32) - 0.5
    return values.astype(jnp.bfloat16)


def block_levels(key, dims, split, low, high):
    def one(axis_at, shards_of):
        steps = jax.random.uniform(jax.random.fold_in(jax.random.fold_in(key, 6), axis_at), (shards_of,), jnp.float32, low / len(split), high / len(split))
        return jnp.repeat(jnp.exp(steps), dims[axis_at] // shards_of).reshape((-1,) + (1,) * (len(dims) - axis_at - 1))

    loudness = one(*split[0])
    for cut in split[1:]:
        loudness = loudness * one(*cut)
    return loudness


def noise(own_key, shape, deviation, bound, split=(), held_as=jnp.bfloat16):
    gain = block_levels(own_key, shape, split, -0.22, 0.18) if split else 1.0
    values = jax.random.normal(own_key, shape, jnp.float32) * deviation * gain
    return jnp.minimum(jnp.maximum(values, -bound), bound).astype(held_as)


def setup_inputs(seed: int = 0) -> dict:
    streams_of = jax.random.split(jax.random.key(seed), 7)
    return {
        "query_in": noise(streams_of[0], (TOKENS, HEADS * DH), 1.0, 6.0, ((0, 16), (1, 16))),
        "key_in": noise(streams_of[1], (TOKENS, HEADS * DH), 1.0, 6.0, ((0, 16), (1, 16))),
        "value_in": draw_value_in(jax.random.fold_in(streams_of[6], 71), 0),
        "gate_in": noise(streams_of[3], (TOKENS, HEADS * DH), 1.5, 6.0, ((0, 16), (1, 16))),
        "norm_gain": jnp.clip(1.0 + 0.18 * jax.random.normal(streams_of[4], (HEADS * DH,), jnp.float32), 0.1, 1.9),
        "head_owner": jax.random.permutation(streams_of[5], N_GRP).astype(jnp.int32),
    }


def activate(arr):
    return jax.nn.silu(arr.astype(jnp.float32)).astype(jnp.bfloat16)

def reference(query_in, key_in, value_in, gate_in, norm_gain, head_owner):
    head_total = HEADS_DEV * N_GRP
    block_len = math.gcd(256, TOKENS)
    block_count = TOKENS // block_len
    causal = (jnp.arange(block_len, dtype=jnp.int32)[:, None] >= jnp.arange(block_len, dtype=jnp.int32)[None, :]).astype(jnp.float32)

    def one_head(head_idx):

        def column_of(arr):
            return lax.dynamic_slice_in_dim(arr, head_idx * DH, DH, arr.ndim - 1)
        q_act = activate(column_of(query_in)).reshape(block_count, block_len, DH)
        k_act = activate(column_of(key_in)).reshape(block_count, block_len, DH)
        v_act = activate(column_of(value_in)).reshape(block_count, block_len, DH)

        def advance(state, blocks):
            q_blk, k_blk, v_blk = blocks
            scores = (jnp.dot(q_blk, k_blk.T, preferred_element_type=jnp.float32) * causal).astype(jnp.bfloat16)
            state_hi = state.astype(jnp.bfloat16)
            state_lo = (state - state_hi.astype(jnp.float32)).astype(jnp.bfloat16)
            result = jnp.dot(scores, v_blk, preferred_element_type=jnp.float32)
            result = result + jnp.dot(q_blk, state_hi, preferred_element_type=jnp.float32)
            result = result + jnp.dot(q_blk, state_lo, preferred_element_type=jnp.float32)
            state = state + jnp.dot(k_blk.T, v_blk, preferred_element_type=jnp.float32)
            return (state, result)
        final_state, outputs = lax.scan(advance, jnp.zeros((DH, DH), jnp.float32), (q_act, k_act, v_act))
        return (outputs.reshape(TOKENS, DH), final_state)
    attn_all, states = lax.map(one_head, jnp.arange(head_total, dtype=jnp.int32))
    squares = lax.optimization_barrier(jnp.sum(attn_all * attn_all, axis=(0, 2))) / (head_total * DH)
    scale = lax.rsqrt(squares + 1e-06)
    attn = jnp.transpose(attn_all, (1, 0, 2)).reshape(TOKENS, head_total * DH)
    normed = attn * scale[:, None] * norm_gain * jax.nn.sigmoid(gate_in.astype(jnp.float32))
    attn_out = normed.astype(jnp.bfloat16)
    grouped = states.reshape(N_GRP, HEADS_DEV, DH, DH)
    decode_state = jnp.zeros_like(grouped).at[head_owner].set(grouped).reshape(head_total, DH, DH)
    return (attn_out, decode_state)
```

```python
import functools

import jax
import jax.numpy as jnp
from jax import lax
from jax.experimental import pallas as pl
from jax.experimental.pallas import tpu as pltpu
from jax.sharding import PartitionSpec as P

DH = 128
F32 = jnp.float32
BF16 = jnp.bfloat16
MIB = 1 << 20


def dot(a, b, dims):
    return lax.dot_general(a, b, (dims, ((), ())), preferred_element_type=F32)


def silu(x):
    half = x.astype(F32) * 0.5
    return (half + half * jnp.tanh(half)).astype(BF16)


def params(mib):
    return pltpu.CompilerParams(vmem_limit_bytes=mib * MIB)


def cost(flops, nbytes, trans=0):
    return pl.CostEstimate(flops=flops, bytes_accessed=nbytes, transcendentals=trans)


def state_kernel(heads, shards, k_ref, v_ref, out_ref, acc):
    step = pl.program_id(0)

    @pl.when(step == 0)
    def _():
        acc[...] = jnp.zeros_like(acc)

    for h in range(heads):
        cols = slice(h * DH, (h + 1) * DH)
        k = silu(k_ref[:, cols])
        v = silu(v_ref[:, cols])
        acc[h] += dot(k, v, ((0,), (0,)))

    @pl.when(step == pl.num_programs(0) - 1)
    def _():
        rows = DH // shards
        for j in range(shards):
            for h in range(heads):
                out_ref[j, h] = acc[h, j * rows : (j + 1) * rows]


def prefix_kernel(shards, part_ref, before_ref, total_ref):
    run = jnp.zeros(part_ref.shape[1:], F32)
    for j in range(shards):
        before_ref[j] = run
        run = run + part_ref[j]
    total_ref[...] = run


def inside_kernel(heads, q_ref, k_ref, v_ref, base_ref, qa_ref, run):
    step = pl.program_id(0)

    @pl.when(step == 0)
    def _():
        run[...] = jnp.zeros_like(run)

    n = q_ref.shape[0]
    causal = lax.broadcasted_iota(jnp.int32, (n, n), 0) >= lax.broadcasted_iota(
        jnp.int32, (n, n), 1
    )
    for h in range(heads):
        cols = slice(h * DH, (h + 1) * DH)
        q = silu(q_ref[:, cols])
        k = silu(k_ref[:, cols])
        v = silu(v_ref[:, cols])
        scores = jnp.where(causal, dot(q, k, ((1,), (1,))), 0.0).astype(BF16)
        state = run[h]
        hi = state.astype(BF16)
        lo = (state - hi.astype(F32)).astype(BF16)
        left = jnp.concatenate([scores, q, q], axis=1)
        right = jnp.concatenate([v, hi, lo], axis=0)
        base_ref[:, cols] = dot(left, right, ((1,), (0,)))
        qa_ref[:, cols] = q
        run[h] = state + dot(k, v, ((0,), (0,)))


def carry_kernel(
    heads, shards, owner_ref, base0_ref, base1_ref, qa0_ref, qa1_ref, before_ref, total_ref,
    attn_ref, send_ref, states, squares,
):
    step = pl.program_id(0)
    groups = send_ref.shape[0]
    half = heads // 2

    @pl.when(step == 0)
    def _():
        for h in range(heads):
            state = before_ref[:, h].reshape(DH, DH)
            hi = state.astype(BF16)
            states[h, :DH] = hi
            states[h, DH:] = (state - hi.astype(F32)).astype(BF16)

    sums = None
    for h in range(heads):
        cols = slice((h % half) * DH, (h % half + 1) * DH)
        base_ref, qa_ref = (base0_ref, qa0_ref) if h < half else (base1_ref, qa1_ref)
        q = qa_ref[:, cols]
        attn = base_ref[:, cols] + dot(
            jnp.concatenate([q, q], axis=1), states[h], ((1,), (0,))
        )
        attn_ref[:, h * DH : (h + 1) * DH] = attn
        sums = attn * attn if sums is None else sums + attn * attn
    tokens = sums.shape[0]
    for c in range(tokens // DH):
        column = jnp.sum(sums[c * DH : (c + 1) * DH], axis=1, keepdims=True)
        row = jnp.transpose(jnp.broadcast_to(column, (DH, DH)))[:1]
        squares[pl.ds(step * (tokens // DH) + c, 1), :] = row

    @pl.when(step == pl.num_programs(0) - 1)
    def _():
        token_rows = squares.shape[0]
        owner = owner_ref[lax.axis_index("grp")]
        mine = squares[...]
        rows = total_ref.shape[1]
        for g in range(groups):
            send_ref[g, :token_rows] = mine
            for h in range(heads):
                at = token_rows + h * rows
                send_ref[g, at : at + rows] = jnp.where(owner == g, total_ref[h], 0.0)


def gate_kernel(attn_ref, gate_ref, gain_ref, out_ref):
    sigmoid = 0.5 + 0.5 * jnp.tanh(gate_ref[...].astype(F32) * 0.5)
    out_ref[...] = attn_ref[...] * (gain_ref[...] * sigmoid)


def norm_kernel(heads, features, got_ref, gated_ref, out_ref, state_ref, scales):
    step = pl.program_id(0)
    groups = got_ref.shape[0]

    @pl.when(step == 0)
    def _():
        total = got_ref[0]
        for g in range(1, groups):
            total = total + got_ref[g]
        token_rows = scales.shape[0]
        scales[...] = lax.rsqrt(total[:token_rows] / features + 1e-6)
        rows = state_ref.shape[1]
        for h in range(heads):
            at = token_rows + h * rows
            state_ref[h] = total[at : at + rows]

    tokens = gated_ref.shape[0]
    for c in range(tokens // DH):
        row = scales[pl.ds(step * (tokens // DH) + c, 1), :]
        column = jnp.transpose(jnp.broadcast_to(row, (DH, DH)))[:, :1]
        part = slice(c * DH, (c + 1) * DH)
        out_ref[part, :] = (gated_ref[part, :] * column).astype(BF16)


def body(query_in, key_in, value_in, gate_in, norm_gain, head_owner):
    tokens, width = query_in.shape
    heads = width // DH
    half = heads // 2
    shards = lax.axis_size("seq")
    groups = lax.axis_size("grp")
    block = min(256, tokens)
    blocks = tokens // block
    rows = DH // shards
    token_rows = tokens // DH
    whole = lambda *shape: pl.BlockSpec(shape, lambda i: (0,) * len(shape))

    big = 2 * block
    part = pl.pallas_call(
        functools.partial(state_kernel, heads, shards),
        grid=(tokens // big,),
        in_specs=[pl.BlockSpec((big, width), lambda i: (i, 0))] * 2,
        out_specs=whole(shards, heads, rows, DH),
        out_shape=jax.ShapeDtypeStruct((shards, heads, rows, DH), F32),
        scratch_shapes=[pltpu.VMEM((heads, DH, DH), F32)],
        compiler_params=params(56),
        cost_estimate=cost(2 * tokens * width * DH, 4 * tokens * width),
        name="local_state",
    )(key_in, value_in)

    gathered = lax.all_to_all(part, "seq", 0, 0, tiled=True)

    def inside(pair):
        spec = pl.BlockSpec((block, half * DH), lambda i: (i, pair))
        out = pl.BlockSpec((block, half * DH), lambda i: (i, 0))
        return pl.pallas_call(
            functools.partial(inside_kernel, half),
            grid=(blocks,),
            in_specs=[spec] * 3,
            out_specs=[out] * 2,
            out_shape=[
                jax.ShapeDtypeStruct((tokens, half * DH), F32),
                jax.ShapeDtypeStruct((tokens, half * DH), BF16),
            ],
            scratch_shapes=[pltpu.VMEM((half, DH, DH), F32)],
            compiler_params=params(56),
            cost_estimate=cost(
                2 * tokens * half * DH * (2 * block + 3 * DH), 12 * tokens * half * DH
            ),
            name="inside%d" % pair,
        )(query_in, key_in, value_in)

    base0, qa0 = inside(0)
    base1, qa1 = inside(1)

    before_all, total = pl.pallas_call(
        functools.partial(prefix_kernel, shards),
        in_specs=[pl.BlockSpec(memory_space=pltpu.VMEM)],
        out_specs=[pl.BlockSpec(memory_space=pltpu.VMEM)] * 2,
        out_shape=[
            jax.ShapeDtypeStruct((shards, heads, rows, DH), F32),
            jax.ShapeDtypeStruct((heads, rows, DH), F32),
        ],
        compiler_params=params(4),
        name="prefix",
    )(gathered)
    before = lax.all_to_all(before_all, "seq", 0, 0, tiled=True)

    pair_spec = pl.BlockSpec((big, half * DH), lambda i: (i, 0))
    payload = token_rows + heads * rows
    attn, send = pl.pallas_call(
        functools.partial(carry_kernel, heads, shards),
        grid=(tokens // big,),
        in_specs=[
            pl.BlockSpec(memory_space=pltpu.SMEM),
            pair_spec, pair_spec, pair_spec, pair_spec,
            whole(shards, heads, rows, DH),
            whole(heads, rows, DH),
        ],
        out_specs=[
            pl.BlockSpec((big, width), lambda i: (i, 0)),
            whole(groups, payload, DH),
        ],
        out_shape=[
            jax.ShapeDtypeStruct((tokens, width), F32),
            jax.ShapeDtypeStruct((groups, payload, DH), F32),
        ],
        scratch_shapes=[
            pltpu.VMEM((heads, 2 * DH, DH), BF16),
            pltpu.VMEM((token_rows, DH), F32),
        ],
        compiler_params=params(56),
        cost_estimate=cost(4 * tokens * width * DH, 10 * tokens * width),
        name="carry",
    )(head_owner, base0, base1, qa0, qa1, before, total)

    got = lax.all_to_all(send, "grp", 0, 0, tiled=True)

    row_spec = pl.BlockSpec((big, width), lambda i: (i, 0))
    gated = pl.pallas_call(
        gate_kernel,
        grid=(tokens // big,),
        in_specs=[row_spec, row_spec, whole(1, width)],
        out_specs=row_spec,
        out_shape=jax.ShapeDtypeStruct((tokens, width), F32),
        compiler_params=params(56),
        cost_estimate=cost(4 * tokens * width, 10 * tokens * width),
        name="gate",
    )(attn, gate_in, norm_gain.reshape(1, width))

    attn_out, decode_state = pl.pallas_call(
        functools.partial(norm_kernel, heads, float(width * groups)),
        grid=(tokens // big,),
        in_specs=[whole(groups, payload, DH), row_spec],
        out_specs=[row_spec, whole(heads, rows, DH)],
        out_shape=[
            jax.ShapeDtypeStruct((tokens, width), BF16),
            jax.ShapeDtypeStruct((heads, rows, DH), F32),
        ],
        scratch_shapes=[pltpu.VMEM((token_rows, DH), F32)],
        compiler_params=params(56),
        cost_estimate=cost(2 * tokens * width, 6 * tokens * width),
        name="norm",
    )(got, gated)
    return attn_out, decode_state


def solution(mesh):
    return jax.shard_map(
        body,
        mesh=mesh,
        in_specs=(
            P("seq", "grp"),
            P("seq", "grp"),
            P("seq", "grp"),
            P("seq", "grp"),
            P("grp"),
            P(),
        ),
        out_specs=(P("seq", "grp"), P("grp", "seq", None)),
        check_vma=False,
    )
```

```python
import functools

import jax
import jax.numpy as jnp
from jax import lax
from jax.experimental import pallas as pl
from jax.experimental.pallas import tpu as pltpu
from jax.sharding import PartitionSpec as P

DH = 128
F32 = jnp.float32
BF16 = jnp.bfloat16
MIB = 1 << 20
VMEM = pl.BlockSpec(memory_space=pltpu.VMEM)
SMEM = pl.BlockSpec(memory_space=pltpu.SMEM)
HBM = pl.BlockSpec(memory_space=pltpu.HBM)


def dot(a, b, dims):
    return lax.dot_general(a, b, (dims, ((), ())), preferred_element_type=F32)


def silu(x):
    half = x.astype(F32) * 0.5
    return (half + half * jnp.tanh(half)).astype(BF16)


def params(mib):
    return pltpu.CompilerParams(vmem_limit_bytes=mib * MIB)


def cost(flops, nbytes, trans=0):
    return pl.CostEstimate(flops=flops, bytes_accessed=nbytes, transcendentals=trans)


def in_hbm(x):
    return pltpu.with_memory_space_constraint(x, pltpu.HBM)


def cols_of(h):
    return slice(h * DH, (h + 1) * DH)


def state_kernel(heads, chunk, k_hbm, v_hbm, ka_ref, va_ref, give_ref, mine_ref, k_in, v_in, acc, sems):
    count = k_in.shape[0] // chunk
    copies = []
    for c in range(count):
        part = pl.ds(c * chunk, chunk)
        pair = [
            pltpu.make_async_copy(k_hbm.at[part], k_in.at[part], sems.at[0, c]),
            pltpu.make_async_copy(v_hbm.at[part], v_in.at[part], sems.at[1, c]),
        ]
        for copy in pair:
            copy.start()
        copies.append(pair)
    for c in range(count):
        part = slice(c * chunk, (c + 1) * chunk)
        for copy in copies[c]:
            copy.wait()
        for h in range(heads):
            k = silu(k_in[part, cols_of(h)])
            v = silu(v_in[part, cols_of(h)])
            ka_ref[part, cols_of(h)] = k
            va_ref[part, cols_of(h)] = v
            new = dot(k, v, ((0,), (0,)))
            acc[h] = new if c == 0 else acc[h] + new
    half = heads // 2
    core = lax.rem(lax.axis_index("seq"), 2)
    for i in range(half):
        give_ref[i] = acc[(1 - core) * half + i]
        mine_ref[i] = acc[core * half + i]


def pair_kernel(mine_ref, other_ref, out_ref):
    out_ref[...] = mine_ref[...] + other_ref[...]


def along_x_kernel(chips, own_ref, *refs):
    got, (before_ref, all_ref) = refs[: chips - 1], refs[chips - 1 :]
    x = lax.rem(lax.div(lax.axis_index("seq"), 2), chips)
    total = own_ref[...]
    before = jnp.zeros_like(total)
    for back in range(1, chips):
        part = got[back - 1][...]
        total = total + part
        before = before + jnp.where(x >= back, part, 0.0)
    before_ref[...] = before
    all_ref[...] = total


def along_y_kernel(chips, before_ref, all_ref, over_ref, mine_ref, other_ref, keep_ref, send_ref):
    at = lax.axis_index("seq")
    core = lax.rem(at, 2)
    y = lax.div(at, 2 * chips)
    before = before_ref[...] + jnp.where(y > 0, over_ref[...], 0.0)
    keep_ref[:, :DH] = before + jnp.where(core > 0, other_ref[...], 0.0)
    send_ref[:, :DH] = before + jnp.where(core > 0, 0.0, mine_ref[...])
    rows = keep_ref.shape[1] - DH
    partner = at + 1 - 2 * core
    for i in range(keep_ref.shape[0]):
        for ref, place in ((keep_ref, at), (send_ref, partner)):
            some = pl.ds(pl.multiple_of(place * rows, 8), rows)
            ref[i, DH:] = all_ref[i, some] + over_ref[i, some]


def inside_kernel(first, heads, block, q_hbm, ka_ref, va_ref, run_in, base_ref, qa_ref, run_ref, q_in, sems):
    count = q_in.shape[0] // block

    def copy(n):
        return pltpu.make_async_copy(
            q_hbm.at[pl.ds((first + n) * block, block)], q_in.at[pl.ds(n * block, block)], sems.at[n]
        )

    for n in range(count):
        copy(n).start()
    run_ref[...] = run_in[...]
    causal = lax.broadcasted_iota(jnp.int32, (block, block), 0) >= lax.broadcasted_iota(
        jnp.int32, (block, block), 1
    )

    @pl.loop(0, count)
    def _(n):
        copy(n).wait()
        part = pl.ds(pl.multiple_of(n * block, block), block)
        whole = pl.ds(pl.multiple_of((first + n) * block, block), block)
        for h in range(heads):
            q = silu(q_in[part, cols_of(h)])
            k = ka_ref[whole, cols_of(h)]
            v = va_ref[whole, cols_of(h)]
            scores = jnp.where(causal, dot(q, k, ((1,), (1,))), 0.0).astype(BF16)
            state = run_ref[h]
            hi = state.astype(BF16)
            lo = (state - hi.astype(F32)).astype(BF16)
            left = jnp.concatenate([scores, q, q], axis=1)
            right = jnp.concatenate([v, hi, lo], axis=0)
            base_ref[part, cols_of(h)] = dot(left, right, ((1,), (0,)))
            qa_ref[part, cols_of(h)] = q
            run_ref[h] = state + dot(k, v, ((0,), (0,)))


def gate_kernel(block, gate_hbm, gain_ref, out_ref, gate_in, sems):
    tokens = gate_in.shape[0]
    count = tokens // block

    def copy(n):
        part = pl.ds(n * block, block)
        return pltpu.make_async_copy(gate_hbm.at[part], gate_in.at[part], sems.at[n])

    for n in range(count):
        copy(n).start()

    @pl.loop(0, count)
    def _(n):
        copy(n).wait()
        part = pl.ds(pl.multiple_of(n * block, block), block)
        sigmoid = 0.5 + 0.5 * jnp.tanh(gate_in[part].astype(F32) * 0.5)
        out_ref[part] = gain_ref[...] * sigmoid


def carry_kernel(
    heads, block, owner_ref, base0_ref, base1_ref, qa0_ref, qa1_ref, keep_ref, got_ref, gate_ref,
    gated_ref, send_ref, states, squares,
):
    half = heads // 2
    core = lax.rem(lax.axis_index("seq"), 2)
    for i in range(half):
        for ref, h in ((keep_ref, core * half + i), (got_ref, (1 - core) * half + i)):
            state = ref[i, :DH]
            hi = state.astype(BF16)
            states[h, :DH] = hi
            states[h, DH:] = (state - hi.astype(F32)).astype(BF16)
    ones = jnp.ones((16, 2 * DH), BF16)
    per = block // DH
    first = 0
    for base_ref, qa_ref in ((base0_ref, qa0_ref), (base1_ref, qa1_ref)):

        @pl.loop(0, base_ref.shape[0] // block)
        def _(n):
            part = pl.ds(pl.multiple_of(n * block, block), block)
            whole = pl.ds(pl.multiple_of((first + n) * block, block), block)
            sums = None
            for h in range(heads):
                q = qa_ref[part, cols_of(h)]
                attn = base_ref[part, cols_of(h)] + dot(
                    jnp.concatenate([q, q], axis=1), states[h], ((1,), (0,))
                )
                gated_ref[whole, cols_of(h)] = attn * gate_ref[whole, cols_of(h)]
                sums = attn * attn if sums is None else sums + attn * attn
            hi = sums.astype(BF16)
            lo = (sums - hi.astype(F32)).astype(BF16)
            across = dot(ones, jnp.concatenate([hi, lo], axis=1), ((1,), (1,)))
            for c in range(per):
                squares[pl.ds((first + n) * per + c, 1), :] = across[:1, c * DH : (c + 1) * DH]

        first += base_ref.shape[0] // block

    token_rows = squares.shape[0]
    owner = owner_ref[lax.axis_index("grp")]
    mine = squares[...]
    rows = keep_ref.shape[1] - DH
    low = [jnp.where(core == 0, keep_ref[i, DH:], got_ref[i, DH:]) for i in range(half)]
    high = [jnp.where(core == 0, got_ref[i, DH:], keep_ref[i, DH:]) for i in range(half)]
    for g in range(send_ref.shape[0]):
        send_ref[g, :token_rows] = mine
        for h, final in enumerate(low + high):
            at = token_rows + h * rows
            send_ref[g, at : at + rows] = jnp.where(owner == g, final, 0.0)


def norm_kernel(heads, features, block, got_ref, gated_ref, out_hbm, state_ref, out, scales, sems):
    total = got_ref[0]
    for g in range(1, got_ref.shape[0]):
        total = total + got_ref[g]
    rows = state_ref.shape[1]
    tokens = out.shape[0]
    token_rows = tokens // DH
    scales[...] = jnp.zeros_like(scales)
    scales[:token_rows] = lax.rsqrt(total[:token_rows] / features + 1e-6)
    columns = jnp.transpose(scales[...])
    copies = []
    for n in range(tokens // block):
        for c in range(n * block // DH, (n + 1) * block // DH):
            part = slice(c * DH, (c + 1) * DH)
            out[part] = (gated_ref[part] * columns[:, c : c + 1]).astype(BF16)
        part = pl.ds(n * block, block)
        copies.append(pltpu.make_async_copy(out.at[part], out_hbm.at[part], sems.at[n]))
        copies[-1].start()
    for h in range(heads):
        at = token_rows + h * rows
        state_ref[h] = total[at : at + rows]
    for copy in copies:
        copy.wait()


def body(query_in, key_in, value_in, gate_in, norm_gain, head_owner):
    tokens, width = query_in.shape
    heads = width // DH
    half = heads // 2
    shards = lax.axis_size("seq")
    groups = lax.axis_size("grp")
    chips = 4
    block = min(256, tokens)
    count = tokens // block
    chunk = 2 * block
    rows = DH // shards
    token_rows = tokens // DH
    pair_state = pltpu.VMEM((half, DH, DH), F32)
    dma = lambda *shape: pltpu.SemaphoreType.DMA(shape)
    limit = params(24)

    ka, va, give, mine = pl.pallas_call(
        functools.partial(state_kernel, heads, chunk),
        in_specs=[HBM, HBM],
        out_specs=[VMEM] * 4,
        out_shape=[pltpu.VMEM((tokens, width), BF16)] * 2 + [pair_state] * 2,
        scratch_shapes=[
            pltpu.VMEM((tokens, width), BF16),
            pltpu.VMEM((tokens, width), BF16),
            pltpu.VMEM((heads, DH, DH), F32),
            dma(2, tokens // chunk),
        ],
        compiler_params=limit,
        cost_estimate=cost(2 * tokens * width * DH, 4 * tokens * width),
        name="local_state",
    )(in_hbm(key_in), in_hbm(value_in))

    def swap(x, bit):
        return lax.ppermute(x, "seq", [(i, i ^ bit) for i in range(shards)])

    def on_x(x, k):
        place = lambda i: i - i % (2 * chips) + (i + 2 * k) % (2 * chips)
        return lax.ppermute(x, "seq", [(i, place(i)) for i in range(shards)])

    def inside(first, blocks, q, ka, va, run):
        part = blocks * block
        return pl.pallas_call(
            functools.partial(inside_kernel, first, heads, block),
            in_specs=[HBM, VMEM, VMEM, VMEM],
            out_specs=[VMEM] * 3,
            out_shape=[
                pltpu.VMEM((part, width), F32),
                pltpu.VMEM((part, width), BF16),
                pltpu.VMEM((heads, DH, DH), F32),
            ],
            scratch_shapes=[pltpu.VMEM((part, width), BF16), dma(blocks)],
            compiler_params=limit,
            cost_estimate=cost(2 * part * width * (2 * block + 3 * DH), 12 * part * width),
            name="inside%d" % first,
        )(in_hbm(q), ka, va, run)

    cut = 5 * count // 8
    other = swap(give, 1)
    pair = pl.pallas_call(
        pair_kernel, in_specs=[VMEM] * 2, out_specs=VMEM, out_shape=pair_state,
        compiler_params=limit, name="pair",
    )(mine, other)
    around = [on_x(pair, k) for k in range(1, chips)]
    ka, va, _ = lax.optimization_barrier((ka, va, pair))
    base0, qa0, run = inside(0, cut, query_in, ka, va, jnp.zeros((heads, DH, DH), F32))
    base0, *around = lax.optimization_barrier((base0, *around))
    before_x, all_x = pl.pallas_call(
        functools.partial(along_x_kernel, chips),
        in_specs=[VMEM] * chips, out_specs=[VMEM] * 2, out_shape=[pair_state] * 2,
        compiler_params=limit, name="along_x",
    )(pair, *around)
    over = swap(all_x, 2 * chips)
    run, _ = lax.optimization_barrier((run, all_x))
    base1, qa1, _ = inside(cut, count - cut, query_in, ka, va, run)
    base1, over = lax.optimization_barrier((base1, over))
    keep, send_core = pl.pallas_call(
        functools.partial(along_y_kernel, chips),
        in_specs=[VMEM] * 5, out_specs=[VMEM] * 2,
        out_shape=[pltpu.VMEM((half, DH + rows, DH), F32)] * 2,
        compiler_params=limit, name="along_y",
    )(before_x, all_x, over, mine, other)
    got_core = swap(send_core, 1)

    gate = pl.pallas_call(
        functools.partial(gate_kernel, block),
        in_specs=[HBM, VMEM],
        out_specs=VMEM,
        out_shape=pltpu.VMEM((tokens, width), F32),
        scratch_shapes=[pltpu.VMEM((tokens, width), BF16), dma(count)],
        compiler_params=limit,
        cost_estimate=cost(4 * tokens * width, 6 * tokens * width),
        name="gate",
    )(in_hbm(gate_in), norm_gain.reshape(1, width))

    payload = token_rows + heads * rows
    gated, send = pl.pallas_call(
        functools.partial(carry_kernel, heads, block),
        in_specs=[SMEM] + [VMEM] * 7,
        out_specs=[VMEM] * 2,
        out_shape=[
            pltpu.VMEM((tokens, width), F32),
            pltpu.VMEM((groups, payload, DH), F32),
        ],
        scratch_shapes=[
            pltpu.VMEM((heads, 2 * DH, DH), BF16),
            pltpu.VMEM((token_rows, DH), F32),
        ],
        compiler_params=limit,
        cost_estimate=cost(4 * tokens * width * DH, 10 * tokens * width),
        name="carry",
    )(head_owner, base0, base1, qa0, qa1, keep, got_core, gate)

    got = lax.all_to_all(send, "grp", 0, 0, tiled=True)

    attn_out, decode_state = pl.pallas_call(
        functools.partial(norm_kernel, heads, float(width * groups), block),
        in_specs=[VMEM, VMEM],
        out_specs=[HBM, VMEM],
        out_shape=[
            jax.ShapeDtypeStruct((tokens, width), BF16),
            jax.ShapeDtypeStruct((heads, rows, DH), F32),
        ],
        scratch_shapes=[
            pltpu.VMEM((tokens, width), BF16),
            pltpu.VMEM((DH, DH), F32),
            dma(count),
        ],
        compiler_params=limit,
        cost_estimate=cost(2 * tokens * width, 6 * tokens * width),
        name="norm",
    )(got, gated)
    return attn_out, decode_state


def solution(mesh):
    return jax.shard_map(
        body,
        mesh=mesh,
        in_specs=(
            P("seq", "grp"),
            P("seq", "grp"),
            P("seq", "grp"),
            P("seq", "grp"),
            P("grp"),
            P(),
        ),
        out_specs=(P("seq", "grp"), P("grp", "seq", None)),
        check_vma=False,
    )
```

```python
import functools

import jax
import jax.numpy as jnp
from jax import lax
from jax.experimental import pallas as pl
from jax.experimental.pallas import tpu as pltpu
from jax.sharding import PartitionSpec as P

DH = 128
F32 = jnp.float32
BF16 = jnp.bfloat16
MIB = 1 << 20
VMEM = pl.BlockSpec(memory_space=pltpu.VMEM)
HBM = pl.BlockSpec(memory_space=pltpu.HBM)


def places(groups):
    return list(range(groups))[::-1]


def dot(a, b, dims):
    return lax.dot_general(a, b, (dims, ((), ())), preferred_element_type=F32)


def silu(x):
    half = x.astype(F32) * 0.5
    return (half + half * jnp.tanh(half)).astype(BF16)


def params(mib):
    return pltpu.CompilerParams(vmem_limit_bytes=mib * MIB)


def cost(flops, nbytes, trans=0):
    return pl.CostEstimate(flops=flops, bytes_accessed=nbytes, transcendentals=trans)


def in_hbm(x):
    return pltpu.with_memory_space_constraint(x, pltpu.HBM)


def cols_of(h):
    return slice(h * DH, (h + 1) * DH)


def state_kernel(
    heads, chunk, k_hbm, v_hbm, q_hbm, gate_hbm, owner_hbm,
    ka_ref, va_ref, give_ref, mine_ref, q_ref, gate_ref, owners_ref, k_in, v_in, acc, owner, sems, late,
):
    count = k_in.shape[0] // chunk

    def pair(c):
        part = pl.ds(c * chunk, chunk)
        return [
            pltpu.make_async_copy(k_hbm.at[part], k_in.at[part], sems.at[0, c]),
            pltpu.make_async_copy(v_hbm.at[part], v_in.at[part], sems.at[1, c]),
        ]

    later = [
        pltpu.make_async_copy(q_hbm, q_ref, late.at[0]),
        pltpu.make_async_copy(gate_hbm, gate_ref, late.at[1]),
        pltpu.make_async_copy(owner_hbm, owner, late.at[2]),
    ]
    for c in range(count):
        for copy in pair(c):
            copy.start()
    for copy in later:
        copy.start()
    acc[...] = jnp.zeros_like(acc)

    @pl.loop(0, count)
    def _(c):
        for copy in pair(c):
            copy.wait()
        part = pl.ds(pl.multiple_of(c * chunk, chunk), chunk)
        for h in range(heads):
            k = silu(k_in[part, cols_of(h)])
            v = silu(v_in[part, cols_of(h)])
            ka_ref[part, cols_of(h)] = k
            va_ref[part, cols_of(h)] = v
            acc[h] += dot(k, v, ((0,), (0,)))

    half = heads // 2
    core = lax.rem(lax.axis_index("seq"), 2)
    for i in range(half):
        give_ref[i] = acc[(1 - core) * half + i]
        mine_ref[i] = acc[core * half + i]
    for copy in later:
        copy.wait()
    group = lax.axis_index("grp")
    for at, g in enumerate((group, group + 1 - 2 * lax.rem(group, 2))):
        owners_ref[at] = jnp.full(owners_ref.shape[1:], owner[g], jnp.int32)


def pair_kernel(mine_ref, other_ref, out_ref):
    out_ref[...] = mine_ref[...] + other_ref[...]


def along_x_kernel(chips, own_ref, *refs):
    got, (before_ref, all_ref) = refs[: chips - 1], refs[chips - 1 :]
    x = lax.rem(lax.div(lax.axis_index("seq"), 2), chips)
    total = own_ref[...]
    before = jnp.zeros_like(total)
    for back in range(1, chips):
        part = got[back - 1][...]
        total = total + part
        before = before + jnp.where(x >= back, part, 0.0)
    before_ref[...] = before
    all_ref[...] = total


def along_y_kernel(chips, before_ref, all_ref, over_ref, mine_ref, other_ref, keep_ref, send_ref, hand_ref):
    at = lax.axis_index("seq")
    core = lax.rem(at, 2)
    y = lax.div(at, 2 * chips)
    before = before_ref[...] + jnp.where(y > 0, over_ref[...], 0.0)
    keep_ref[:, :DH] = before + jnp.where(core > 0, other_ref[...], 0.0)
    send_ref[:, :DH] = before + jnp.where(core > 0, 0.0, mine_ref[...])
    rows = keep_ref.shape[1] - DH
    partner = at + 1 - 2 * core
    side = lax.rem(lax.axis_index("grp"), 2)
    for i in range(keep_ref.shape[0]):
        finals = []
        for ref, place in ((keep_ref, at), (send_ref, partner)):
            some = pl.ds(pl.multiple_of(place * rows, 8), rows)
            finals.append(all_ref[i, some] + over_ref[i, some])
            ref[i, DH:] = finals[-1]
        hand_ref[i] = jnp.where(side == 0, finals[1], finals[0])


def inside_kernel(first, heads, block, q_ref, ka_ref, va_ref, run_in, base_ref, qa_ref, run_ref):
    count = qa_ref.shape[0] // block
    run_ref[...] = run_in[...]
    causal = lax.broadcasted_iota(jnp.int32, (block, block), 0) >= lax.broadcasted_iota(
        jnp.int32, (block, block), 1
    )

    @pl.loop(0, count, unroll=2)
    def _(n):
        part = pl.ds(pl.multiple_of(n * block, block), block)
        whole = pl.ds(pl.multiple_of((first + n) * block, block), block)
        for h in range(heads):
            q = silu(q_ref[whole, cols_of(h)])
            k = ka_ref[whole, cols_of(h)]
            v = va_ref[whole, cols_of(h)]
            scores = jnp.where(causal, dot(q, k, ((1,), (1,))), 0.0).astype(BF16)
            state = run_ref[h]
            hi = state.astype(BF16)
            lo = (state - hi.astype(F32)).astype(BF16)
            left = jnp.concatenate([scores, q, q], axis=1)
            right = jnp.concatenate([v, hi, lo], axis=0)
            base_ref[part, cols_of(h)] = dot(left, right, ((1,), (0,)))
            qa_ref[part, cols_of(h)] = q
            run_ref[h] = state + dot(k, v, ((0,), (0,)))


def gate_kernel(gate_ref, gain_ref, out_ref):
    sigmoid = 0.5 + 0.5 * jnp.tanh(gate_ref[...].astype(F32) * 0.5)
    out_ref[...] = gain_ref[...] * sigmoid


def carry_kernel(
    heads, block, base0_ref, base1_ref, qa0_ref, qa1_ref, keep_ref, got_ref, gate_ref,
    gated_ref, mine_ref, states, squares,
):
    half = heads // 2
    core = lax.rem(lax.axis_index("seq"), 2)
    for i in range(half):
        for ref, h in ((keep_ref, core * half + i), (got_ref, (1 - core) * half + i)):
            state = ref[i, :DH]
            hi = state.astype(BF16)
            states[h, :DH] = hi
            states[h, DH:] = (state - hi.astype(F32)).astype(BF16)
    first = 0
    for base_ref, qa_ref in ((base0_ref, qa0_ref), (base1_ref, qa1_ref)):

        @pl.loop(0, base_ref.shape[0] // block, unroll=2)
        def _(n):
            part = pl.ds(pl.multiple_of(n * block, block), block)
            whole = pl.ds(pl.multiple_of((first + n) * block, block), block)
            sums = None
            for h in range(heads):
                q = qa_ref[part, cols_of(h)]
                attn = base_ref[part, cols_of(h)] + dot(
                    jnp.concatenate([q, q], axis=1), states[h], ((1,), (0,))
                )
                gated_ref[whole, cols_of(h)] = attn * gate_ref[whole, cols_of(h)]
                sums = attn * attn if sums is None else sums + attn * attn
            hi = sums.astype(BF16)
            squares[whole, :DH] = hi
            squares[whole, DH:] = (sums - hi.astype(F32)).astype(BF16)

        first += base_ref.shape[0] // block

    across = dot(jnp.ones((16, 2 * DH), BF16), squares[...], ((1,), (1,)))
    for c in range(squares.shape[0] // DH):
        mine_ref[c : c + 1] = across[:1, cols_of(c)]


def pack_kernel(owners_ref, squares_ref, keep_ref, got_ref, handed_ref, send_ref):
    side = lax.rem(lax.axis_index("grp"), 2)
    token_rows = squares_ref.shape[0]
    half, rows, _ = handed_ref.shape
    own, other = owners_ref[0], owners_ref[1]
    for place, g in enumerate(places(send_ref.shape[0])):
        send_ref[place, :token_rows] = squares_ref[...]
        for i in range(half):
            at = token_rows + i * rows
            final = jnp.where(side == 0, keep_ref[i, DH:], got_ref[i, DH:])
            send_ref[place, at : at + rows] = jnp.where(
                own == g, final, jnp.where(other == g, handed_ref[i], 0.0)
            )


def norm_kernel(heads, features, block, got_ref, gated_ref, out_hbm, state_ref, out, scales, sems):
    sums = [None, None]
    for place, g in enumerate(places(got_ref.shape[0])):
        sums[g % 2] = got_ref[place] if sums[g % 2] is None else sums[g % 2] + got_ref[place]
    even, odd = sums
    rows = state_ref.shape[1]
    tokens = out.shape[0]
    token_rows = tokens // DH
    scales[...] = jnp.zeros_like(scales)
    scales[:token_rows] = lax.rsqrt(
        (even[:token_rows] + odd[:token_rows]) / features + 1e-6
    )
    columns = jnp.transpose(scales[...])
    copies = []
    for n in range(tokens // block):
        for c in range(n * block // DH, (n + 1) * block // DH):
            part = slice(c * DH, (c + 1) * DH)
            out[part] = (gated_ref[part] * columns[:, c : c + 1]).astype(BF16)
        part = pl.ds(n * block, block)
        copies.append(pltpu.make_async_copy(out.at[part], out_hbm.at[part], sems.at[n]))
        copies[-1].start()
    half = heads // 2
    core = lax.rem(lax.axis_index("seq"), 2)
    for i in range(half):
        at = token_rows + i * rows
        state_ref[core * half + i] = even[at : at + rows]
        state_ref[(1 - core) * half + i] = odd[at : at + rows]
    for copy in copies:
        copy.wait()


def body(query_in, key_in, value_in, gate_in, norm_gain, head_owner):
    tokens, width = query_in.shape
    heads = width // DH
    half = heads // 2
    shards = lax.axis_size("seq")
    groups = lax.axis_size("grp")
    chips = 4
    block = min(256, tokens)
    count = tokens // block
    chunk = 2 * block
    rows = DH // shards
    token_rows = tokens // DH
    wide = pltpu.VMEM((tokens, width), BF16)
    pair_state = pltpu.VMEM((half, DH, DH), F32)
    dma = lambda *shape: pltpu.SemaphoreType.DMA(shape)
    limit = params(24)

    ka, va, give, mine, query, gate, owners = pl.pallas_call(
        functools.partial(state_kernel, heads, chunk),
        in_specs=[HBM] * 5,
        out_specs=[VMEM] * 7,
        out_shape=[wide] * 2 + [pair_state] * 2 + [wide] * 2
        + [pltpu.VMEM((2, rows, DH), jnp.int32)],
        scratch_shapes=[
            pltpu.VMEM((tokens, width), BF16),
            pltpu.VMEM((tokens, width), BF16),
            pltpu.VMEM((heads, DH, DH), F32),
            pltpu.SMEM(head_owner.shape, jnp.int32),
            dma(2, tokens // chunk),
            dma(3),
        ],
        compiler_params=limit,
        cost_estimate=cost(2 * tokens * width * DH, 4 * tokens * width),
        name="local_state",
    )(in_hbm(key_in), in_hbm(value_in), in_hbm(query_in), in_hbm(gate_in), in_hbm(head_owner))

    def swap(x, bit):
        return lax.ppermute(x, "seq", [(i, i ^ bit) for i in range(shards)])

    def on_x(x, k):
        place = lambda i: i - i % (2 * chips) + (i + 2 * k) % (2 * chips)
        return lax.ppermute(x, "seq", [(i, place(i)) for i in range(shards)])

    def inside(first, blocks, q, ka, va, run):
        part = blocks * block
        return pl.pallas_call(
            functools.partial(inside_kernel, first, heads, block),
            in_specs=[VMEM] * 4,
            out_specs=[VMEM] * 3,
            out_shape=[
                pltpu.VMEM((part, width), F32),
                pltpu.VMEM((part, width), BF16),
                pltpu.VMEM((heads, DH, DH), F32),
            ],
            compiler_params=limit,
            cost_estimate=cost(2 * part * width * (2 * block + 3 * DH), 12 * part * width),
            name="inside%d" % first,
        )(q, ka, va, run)

    cut = 6 * count // 8
    other = swap(give, 1)
    pair = pl.pallas_call(
        pair_kernel, in_specs=[VMEM] * 2, out_specs=VMEM, out_shape=pair_state,
        compiler_params=limit, name="pair",
    )(mine, other)
    around = [on_x(pair, k) for k in range(1, chips)]
    ka, va, _ = lax.optimization_barrier((ka, va, pair))
    base0, qa0, run = inside(0, cut, query, ka, va, jnp.zeros((heads, DH, DH), F32))
    base0, *around = lax.optimization_barrier((base0, *around))
    before_x, all_x = pl.pallas_call(
        functools.partial(along_x_kernel, chips),
        in_specs=[VMEM] * chips, out_specs=[VMEM] * 2, out_shape=[pair_state] * 2,
        compiler_params=limit, name="along_x",
    )(pair, *around)
    over = swap(all_x, 2 * chips)
    run, _ = lax.optimization_barrier((run, all_x))
    base1, qa1, _ = inside(cut, count - cut, query, ka, va, run)
    gate, _ = lax.optimization_barrier((gate, all_x))
    gate = pl.pallas_call(
        gate_kernel,
        in_specs=[VMEM, VMEM],
        out_specs=VMEM,
        out_shape=pltpu.VMEM((tokens, width), F32),
        compiler_params=limit,
        cost_estimate=cost(4 * tokens * width, 6 * tokens * width),
        name="gate",
    )(gate, norm_gain.reshape(1, width))

    base1, gate, over = lax.optimization_barrier((base1, gate, over))
    keep, send_core, hand = pl.pallas_call(
        functools.partial(along_y_kernel, chips),
        in_specs=[VMEM] * 5, out_specs=[VMEM] * 3,
        out_shape=[pltpu.VMEM((half, DH + rows, DH), F32)] * 2
        + [pltpu.VMEM((half, rows, DH), F32)],
        compiler_params=limit, name="along_y",
    )(before_x, all_x, over, mine, other)
    got_core = swap(send_core, 1)
    crossing = [
        (i * groups + g, (i if g % 2 else i ^ 1) * groups + (g ^ 1))
        for i in range(shards)
        for g in range(groups)
    ]
    handed = lax.ppermute(hand, ("seq", "grp"), crossing)

    payload = token_rows + half * rows
    gated, squares = pl.pallas_call(
        functools.partial(carry_kernel, heads, block),
        in_specs=[VMEM] * 7,
        out_specs=[VMEM] * 2,
        out_shape=[
            pltpu.VMEM((tokens, width), F32),
            pltpu.VMEM((token_rows, DH), F32),
        ],
        scratch_shapes=[
            pltpu.VMEM((heads, 2 * DH, DH), BF16),
            pltpu.VMEM((tokens, 2 * DH), BF16),
        ],
        compiler_params=limit,
        cost_estimate=cost(4 * tokens * width * DH, 10 * tokens * width),
        name="carry",
    )(base0, base1, qa0, qa1, keep, got_core, gate)

    send = pl.pallas_call(
        pack_kernel,
        in_specs=[VMEM] * 5,
        out_specs=VMEM,
        out_shape=pltpu.VMEM((groups, payload, DH), F32),
        compiler_params=limit,
        name="pack",
    )(owners, squares, keep, got_core, handed)

    got = lax.all_to_all(
        send, "grp", 0, 0, tiled=True, axis_index_groups=[places(groups)]
    )

    attn_out, decode_state = pl.pallas_call(
        functools.partial(norm_kernel, heads, float(width * groups), block),
        in_specs=[VMEM, VMEM],
        out_specs=[HBM, VMEM],
        out_shape=[
            jax.ShapeDtypeStruct((tokens, width), BF16),
            jax.ShapeDtypeStruct((heads, rows, DH), F32),
        ],
        scratch_shapes=[
            pltpu.VMEM((tokens, width), BF16),
            pltpu.VMEM((DH, DH), F32),
            dma(count),
        ],
        compiler_params=limit,
        cost_estimate=cost(2 * tokens * width, 6 * tokens * width),
        name="norm",
    )(got, gated)
    return attn_out, decode_state


def solution(mesh):
    return jax.shard_map(
        body,
        mesh=mesh,
        in_specs=(
            P("seq", "grp"),
            P("seq", "grp"),
            P("seq", "grp"),
            P("seq", "grp"),
            P("grp"),
            P(),
        ),
        out_specs=(P("seq", "grp"), P("grp", "seq", None)),
        check_vma=False,
    )
```

```python
import functools

import jax
import jax.numpy as jnp
from jax import lax
from jax.experimental import pallas as pl
from jax.experimental.pallas import tpu as pltpu
from jax.sharding import PartitionSpec as P

DH = 128
F32 = jnp.float32
BF16 = jnp.bfloat16
MIB = 1 << 20
VMEM = pl.BlockSpec(memory_space=pltpu.VMEM)
HBM = pl.BlockSpec(memory_space=pltpu.HBM)


def lines(groups):
    return [list(range(groups - 2 + side, -1, -2)) for side in range(2)]


def dot(a, b, dims):
    return lax.dot_general(a, b, (dims, ((), ())), preferred_element_type=F32)


def silu(x):
    half = x.astype(F32) * 0.5
    return (half + half * jnp.tanh(half)).astype(BF16)


def params(mib):
    return pltpu.CompilerParams(vmem_limit_bytes=mib * MIB)


def cost(flops, nbytes, trans=0):
    return pl.CostEstimate(flops=flops, bytes_accessed=nbytes, transcendentals=trans)


def in_hbm(x):
    return pltpu.with_memory_space_constraint(x, pltpu.HBM)


def cols_of(h):
    return slice(h * DH, (h + 1) * DH)


def state_kernel(
    heads, chunk, k_hbm, v_hbm, q_hbm, gate_hbm, owner_hbm,
    ka_ref, va_ref, give_ref, mine_ref, q_ref, gate_ref, owners_ref, k_in, v_in, acc, owner, sems, late,
):
    count = k_in.shape[0] // chunk

    def pair(c):
        part = pl.ds(c * chunk, chunk)
        return [
            pltpu.make_async_copy(k_hbm.at[part], k_in.at[part], sems.at[0, c]),
            pltpu.make_async_copy(v_hbm.at[part], v_in.at[part], sems.at[1, c]),
        ]

    later = [
        pltpu.make_async_copy(q_hbm, q_ref, late.at[0]),
        pltpu.make_async_copy(gate_hbm, gate_ref, late.at[1]),
        pltpu.make_async_copy(owner_hbm, owner, late.at[2]),
    ]
    for c in range(count):
        for copy in pair(c):
            copy.start()
    for copy in later:
        copy.start()
    acc[...] = jnp.zeros_like(acc)

    @pl.loop(0, count)
    def _(c):
        for copy in pair(c):
            copy.wait()
        part = pl.ds(pl.multiple_of(c * chunk, chunk), chunk)
        for h in range(heads):
            k = silu(k_in[part, cols_of(h)])
            v = silu(v_in[part, cols_of(h)])
            ka_ref[part, cols_of(h)] = k
            va_ref[part, cols_of(h)] = v
            acc[h] += dot(k, v, ((0,), (0,)))

    half = heads // 2
    core = lax.rem(lax.axis_index("seq"), 2)
    for i in range(half):
        give_ref[i] = acc[(1 - core) * half + i]
        mine_ref[i] = acc[core * half + i]
    for copy in later:
        copy.wait()
    group = lax.axis_index("grp")
    for at, g in enumerate((group, group + 1 - 2 * lax.rem(group, 2))):
        owners_ref[at] = jnp.full(owners_ref.shape[1:], owner[g], jnp.int32)


def pair_kernel(mine_ref, other_ref, out_ref):
    out_ref[...] = mine_ref[...] + other_ref[...]


def along_x_kernel(chips, own_ref, *refs):
    got, (before_ref, all_ref) = refs[: chips - 1], refs[chips - 1 :]
    x = lax.rem(lax.div(lax.axis_index("seq"), 2), chips)
    total = own_ref[...]
    before = jnp.zeros_like(total)
    for back in range(1, chips):
        part = got[chips - 1 - back][...]
        total = total + part
        before = before + jnp.where(x >= back, part, 0.0)
    before_ref[...] = before
    all_ref[...] = total


def along_y_kernel(chips, before_ref, all_ref, over_ref, mine_ref, other_ref, keep_ref, send_ref):
    at = lax.axis_index("seq")
    core = lax.rem(at, 2)
    y = lax.div(at, 2 * chips)
    before = before_ref[...] + jnp.where(y > 0, over_ref[...], 0.0)
    keep_ref[:, :DH] = before + jnp.where(core > 0, other_ref[...], 0.0)
    send_ref[:, :DH] = before + jnp.where(core > 0, 0.0, mine_ref[...])
    rows = keep_ref.shape[1] - DH
    partner = at + 1 - 2 * core
    for i in range(keep_ref.shape[0]):
        for ref, place in ((keep_ref, at), (send_ref, partner)):
            some = pl.ds(pl.multiple_of(place * rows, 8), rows)
            ref[i, DH:] = all_ref[i, some] + over_ref[i, some]


def inside_kernel(first, heads, block, q_ref, ka_ref, va_ref, run_in, base_ref, qa_ref, run_ref):
    count = qa_ref.shape[0] // block
    run_ref[...] = run_in[...]
    causal = lax.broadcasted_iota(jnp.int32, (block, block), 0) >= lax.broadcasted_iota(
        jnp.int32, (block, block), 1
    )

    @pl.loop(0, count, unroll=2)
    def _(n):
        part = pl.ds(pl.multiple_of(n * block, block), block)
        whole = pl.ds(pl.multiple_of((first + n) * block, block), block)
        for h in range(heads):
            q = silu(q_ref[whole, cols_of(h)])
            k = ka_ref[whole, cols_of(h)]
            v = va_ref[whole, cols_of(h)]
            scores = jnp.where(causal, dot(q, k, ((1,), (1,))), 0.0).astype(BF16)
            state = run_ref[h]
            hi = state.astype(BF16)
            lo = (state - hi.astype(F32)).astype(BF16)
            left = jnp.concatenate([scores, q, q], axis=1)
            right = jnp.concatenate([v, hi, lo], axis=0)
            base_ref[part, cols_of(h)] = dot(left, right, ((1,), (0,)))
            qa_ref[part, cols_of(h)] = q
            run_ref[h] = state + dot(k, v, ((0,), (0,)))


def gate_kernel(attn_ref, gate_ref, gain_ref, out_ref):
    sigmoid = 0.5 + 0.5 * jnp.tanh(gate_ref[...].astype(F32) * 0.5)
    out_ref[...] = attn_ref[...] * (gain_ref[...] * sigmoid)


def carry_kernel(
    heads, block, base0_ref, base1_ref, qa0_ref, qa1_ref, keep_ref, got_ref,
    attn_ref, mine_ref, states, squares,
):
    half = heads // 2
    core = lax.rem(lax.axis_index("seq"), 2)
    for i in range(half):
        for ref, h in ((keep_ref, core * half + i), (got_ref, (1 - core) * half + i)):
            state = ref[i, :DH]
            hi = state.astype(BF16)
            states[h, :DH] = hi
            states[h, DH:] = (state - hi.astype(F32)).astype(BF16)
    first = 0
    for base_ref, qa_ref in ((base0_ref, qa0_ref), (base1_ref, qa1_ref)):

        @pl.loop(0, base_ref.shape[0] // block, unroll=2)
        def _(n):
            part = pl.ds(pl.multiple_of(n * block, block), block)
            whole = pl.ds(pl.multiple_of((first + n) * block, block), block)
            sums = None
            for h in range(heads):
                q = qa_ref[part, cols_of(h)]
                attn = base_ref[part, cols_of(h)] + dot(
                    jnp.concatenate([q, q], axis=1), states[h], ((1,), (0,))
                )
                attn_ref[whole, cols_of(h)] = attn
                sums = attn * attn if sums is None else sums + attn * attn
            hi = sums.astype(BF16)
            squares[whole, :DH] = hi
            squares[whole, DH:] = (sums - hi.astype(F32)).astype(BF16)

        first += base_ref.shape[0] // block

    across = dot(jnp.ones((16, 2 * DH), BF16), squares[...], ((1,), (1,)))
    token_rows = squares.shape[0] // DH
    for c in range(token_rows):
        mine_ref[c : c + 1] = across[:1, cols_of(c)]
    rows = keep_ref.shape[1] - DH
    for i in range(half):
        for ref, h in ((keep_ref, core * half + i), (got_ref, (1 - core) * half + i)):
            mine_ref[pl.ds(pl.multiple_of(token_rows + h * rows, 8), rows)] = ref[i, DH:]


def pack_kernel(owners_ref, mine_ref, other_ref, send_ref):
    side = lax.rem(lax.axis_index("grp"), 2)
    rows = owners_ref.shape[1]
    width = mine_ref.shape[0]
    token_rows = width - 4 * rows
    own, other = owners_ref[0] - side, owners_ref[1] - side
    both = mine_ref[:token_rows] + other_ref[:token_rows]
    for place, g in enumerate(lines(2 * send_ref.shape[0])[0]):
        send_ref[place, :token_rows] = both
        for at in range(token_rows, width, rows):
            part = slice(at, at + rows)
            send_ref[place, part] = jnp.where(
                own == g, mine_ref[part], jnp.where(other == g, other_ref[part], 0.0)
            )


def norm_kernel(heads, features, block, got_ref, gated_ref, out_hbm, state_ref, out, scales, sems):
    total = got_ref[0]
    for place in range(1, got_ref.shape[0]):
        total = total + got_ref[place]
    rows = state_ref.shape[1]
    tokens = out.shape[0]
    token_rows = tokens // DH
    scales[...] = jnp.zeros_like(scales)
    scales[:token_rows] = lax.rsqrt(total[:token_rows] / features + 1e-6)
    columns = jnp.transpose(scales[...])
    copies = []
    for n in range(tokens // block):
        for c in range(n * block // DH, (n + 1) * block // DH):
            part = slice(c * DH, (c + 1) * DH)
            out[part] = (gated_ref[part] * columns[:, c : c + 1]).astype(BF16)
        part = pl.ds(n * block, block)
        copies.append(pltpu.make_async_copy(out.at[part], out_hbm.at[part], sems.at[n]))
        copies[-1].start()
    for h in range(heads):
        at = token_rows + h * rows
        state_ref[h] = total[at : at + rows]
    for copy in copies:
        copy.wait()


def body(query_in, key_in, value_in, gate_in, norm_gain, head_owner):
    tokens, width = query_in.shape
    heads = width // DH
    half = heads // 2
    shards = lax.axis_size("seq")
    groups = lax.axis_size("grp")
    chips = 4
    block = min(256, tokens)
    count = tokens // block
    chunk = 2 * block
    rows = DH // shards
    token_rows = tokens // DH
    wide = pltpu.VMEM((tokens, width), BF16)
    pair_state = pltpu.VMEM((half, DH, DH), F32)
    dma = lambda *shape: pltpu.SemaphoreType.DMA(shape)
    limit = params(24)

    ka, va, give, mine, query, gate, owners = pl.pallas_call(
        functools.partial(state_kernel, heads, chunk),
        in_specs=[HBM] * 5,
        out_specs=[VMEM] * 7,
        out_shape=[wide] * 2 + [pair_state] * 2 + [wide] * 2
        + [pltpu.VMEM((2, rows, DH), jnp.int32)],
        scratch_shapes=[
            pltpu.VMEM((tokens, width), BF16),
            pltpu.VMEM((tokens, width), BF16),
            pltpu.VMEM((heads, DH, DH), F32),
            pltpu.SMEM(head_owner.shape, jnp.int32),
            dma(2, tokens // chunk),
            dma(3),
        ],
        compiler_params=limit,
        cost_estimate=cost(2 * tokens * width * DH, 4 * tokens * width),
        name="local_state",
    )(in_hbm(key_in), in_hbm(value_in), in_hbm(query_in), in_hbm(gate_in), in_hbm(head_owner))

    def swap(x, bit):
        return lax.ppermute(x, "seq", [(i, i ^ bit) for i in range(shards)])

    def on_x(x, k):
        place = lambda i: i - i % (2 * chips) + (i + 2 * k) % (2 * chips)
        return lax.ppermute(x, "seq", [(i, place(i)) for i in range(shards)])

    def inside(first, blocks, q, ka, va, run):
        part = blocks * block
        return pl.pallas_call(
            functools.partial(inside_kernel, first, heads, block),
            in_specs=[VMEM] * 4,
            out_specs=[VMEM] * 3,
            out_shape=[
                pltpu.VMEM((part, width), F32),
                pltpu.VMEM((part, width), BF16),
                pltpu.VMEM((heads, DH, DH), F32),
            ],
            compiler_params=limit,
            cost_estimate=cost(2 * part * width * (2 * block + 3 * DH), 12 * part * width),
            name="inside%d" % first,
        )(q, ka, va, run)

    cut = 5 * count // 8
    other = swap(give, 1)
    pair = pl.pallas_call(
        pair_kernel, in_specs=[VMEM] * 2, out_specs=VMEM, out_shape=pair_state,
        compiler_params=limit, name="pair",
    )(mine, other)
    around = [on_x(pair, k) for k in range(chips - 1, 0, -1)]
    ka, va, _ = lax.optimization_barrier((ka, va, pair))
    base0, qa0, run = inside(0, cut, query, ka, va, jnp.zeros((heads, DH, DH), F32))
    base0, *around = lax.optimization_barrier((base0, *around))
    before_x, all_x = pl.pallas_call(
        functools.partial(along_x_kernel, chips),
        in_specs=[VMEM] * chips, out_specs=[VMEM] * 2, out_shape=[pair_state] * 2,
        compiler_params=limit, name="along_x",
    )(pair, *around)
    over = swap(all_x, 2 * chips)
    run, _ = lax.optimization_barrier((run, all_x))
    base1, qa1, _ = inside(cut, count - cut, query, ka, va, run)
    base1, over = lax.optimization_barrier((base1, over))
    keep, send_core = pl.pallas_call(
        functools.partial(along_y_kernel, chips),
        in_specs=[VMEM] * 5, out_specs=[VMEM] * 2,
        out_shape=[pltpu.VMEM((half, DH + rows, DH), F32)] * 2,
        compiler_params=limit, name="along_y",
    )(before_x, all_x, over, mine, other)
    got_core = swap(send_core, 1)
    payload = token_rows + heads * rows
    attn, own = pl.pallas_call(
        functools.partial(carry_kernel, heads, block),
        in_specs=[VMEM] * 6,
        out_specs=[VMEM] * 2,
        out_shape=[
            pltpu.VMEM((tokens, width), F32),
            pltpu.VMEM((payload, DH), F32),
        ],
        scratch_shapes=[
            pltpu.VMEM((heads, 2 * DH, DH), BF16),
            pltpu.VMEM((tokens, 2 * DH), BF16),
        ],
        compiler_params=limit,
        cost_estimate=cost(4 * tokens * width * DH, 10 * tokens * width),
        name="carry",
    )(base0, base1, qa0, qa1, keep, got_core)

    beside = lax.ppermute(own, "grp", [(g, g ^ 1) for g in range(groups)])
    gated = pl.pallas_call(
        gate_kernel,
        in_specs=[VMEM] * 3,
        out_specs=VMEM,
        out_shape=pltpu.VMEM((tokens, width), F32),
        compiler_params=limit,
        cost_estimate=cost(4 * tokens * width, 10 * tokens * width),
        name="gate",
    )(attn, gate, norm_gain.reshape(1, width))
    gated, beside = lax.optimization_barrier((gated, beside))
    send = pl.pallas_call(
        pack_kernel,
        in_specs=[VMEM] * 3,
        out_specs=VMEM,
        out_shape=pltpu.VMEM((groups // 2, payload, DH), F32),
        compiler_params=limit,
        name="pack",
    )(owners, own, beside)

    got = lax.all_to_all(
        send, "grp", 0, 0, tiled=True, axis_index_groups=lines(groups)
    )

    attn_out, decode_state = pl.pallas_call(
        functools.partial(norm_kernel, heads, float(width * groups), block),
        in_specs=[VMEM, VMEM],
        out_specs=[HBM, VMEM],
        out_shape=[
            jax.ShapeDtypeStruct((tokens, width), BF16),
            jax.ShapeDtypeStruct((heads, rows, DH), F32),
        ],
        scratch_shapes=[
            pltpu.VMEM((tokens, width), BF16),
            pltpu.VMEM((DH, DH), F32),
            dma(count),
        ],
        compiler_params=limit,
        cost_estimate=cost(2 * tokens * width, 6 * tokens * width),
        name="norm",
    )(got, gated)
    return attn_out, decode_state


def solution(mesh):
    return jax.shard_map(
        body,
        mesh=mesh,
        in_specs=(
            P("seq", "grp"),
            P("seq", "grp"),
            P("seq", "grp"),
            P("seq", "grp"),
            P("grp"),
            P(),
        ),
        out_specs=(P("seq", "grp"), P("grp", "seq", None)),
        check_vma=False,
    )
```

```python
import functools

import jax
import jax.numpy as jnp
from jax import lax
from jax.experimental import pallas as pl
from jax.experimental.pallas import tpu as pltpu
from jax.sharding import PartitionSpec as P

DH = 128
F32 = jnp.float32
BF16 = jnp.bfloat16
MIB = 1 << 20
VMEM = pl.BlockSpec(memory_space=pltpu.VMEM)
HBM = pl.BlockSpec(memory_space=pltpu.HBM)


def lines(groups):
    count = groups // 2
    order = [6, 5, 4, 7, 3, 2, 1, 0] if count == 8 else list(range(count))[::-1]
    return [[2 * at + side for at in order] for side in range(2)]


def dot(a, b, dims):
    return lax.dot_general(a, b, (dims, ((), ())), preferred_element_type=F32)


def silu(x):
    half = x.astype(F32) * 0.5
    return (half + half * jnp.tanh(half)).astype(BF16)


def params(mib):
    return pltpu.CompilerParams(vmem_limit_bytes=mib * MIB)


def cost(flops, nbytes, trans=0):
    return pl.CostEstimate(flops=flops, bytes_accessed=nbytes, transcendentals=trans)


def in_hbm(x):
    return pltpu.with_memory_space_constraint(x, pltpu.HBM)


def cols_of(h):
    return slice(h * DH, (h + 1) * DH)


def pair_start(width, own):
    core = lax.rem(lax.axis_index("seq"), 2)
    return pl.multiple_of((core if own else 1 - core) * (width // 2), width // 2)


def add_states(first, part, k_in, v_in, ka_ref, va_ref, state_ref):
    for i in range(state_ref.shape[0]):
        wide = pl.ds(pl.multiple_of(first + i * DH, DH), DH)
        k = silu(k_in[part, wide])
        v = silu(v_in[part, wide])
        ka_ref[part, cols_of(i)] = k
        va_ref[part, cols_of(i)] = v
        state_ref[i] += dot(k, v, ((0,), (0,)))


def give_kernel(chunk, k_hbm, v_hbm, q_hbm, k_in, v_in, q_ref, ka_ref, va_ref, give_ref, sems, late):
    count = k_in.shape[0] // chunk

    def pair(c):
        part = pl.ds(c * chunk, chunk)
        return [
            pltpu.make_async_copy(k_hbm.at[part], k_in.at[part], sems.at[0, c]),
            pltpu.make_async_copy(v_hbm.at[part], v_in.at[part], sems.at[1, c]),
        ]

    later = pltpu.make_async_copy(q_hbm, q_ref, late)
    for c in range(count):
        for copy in pair(c):
            copy.start()
    later.start()
    give_ref[...] = jnp.zeros_like(give_ref)
    first = pair_start(k_in.shape[1], False)

    @pl.loop(0, count)
    def _(c):
        for copy in pair(c):
            copy.wait()
        part = pl.ds(pl.multiple_of(c * chunk, chunk), chunk)
        add_states(first, part, k_in, v_in, ka_ref, va_ref, give_ref)

    later.wait()


def mine_kernel(chunk, k_in, v_in, owner_hbm, ka_ref, va_ref, mine_ref, owners_ref, owner, sem):
    copy = pltpu.make_async_copy(owner_hbm, owner, sem)
    copy.start()
    mine_ref[...] = jnp.zeros_like(mine_ref)
    first = pair_start(k_in.shape[1], True)

    @pl.loop(0, k_in.shape[0] // chunk)
    def _(c):
        part = pl.ds(pl.multiple_of(c * chunk, chunk), chunk)
        add_states(first, part, k_in, v_in, ka_ref, va_ref, mine_ref)

    copy.wait()
    group = lax.axis_index("grp")
    for at, g in enumerate((group, group + 1 - 2 * lax.rem(group, 2))):
        owners_ref[at] = jnp.full(owners_ref.shape[1:], owner[g], jnp.int32)


def pair_kernel(mine_ref, other_ref, out_ref):
    out_ref[...] = mine_ref[...] + other_ref[...]


def along_x_kernel(chips, own_ref, *refs):
    got, (before_ref, all_ref) = refs[: chips - 1], refs[chips - 1 :]
    x = lax.rem(lax.div(lax.axis_index("seq"), 2), chips)
    total = own_ref[...]
    before = jnp.zeros_like(total)
    for back in range(1, chips):
        part = got[chips - 1 - back][...]
        total = total + part
        before = before + jnp.where(x >= back, part, 0.0)
    before_ref[...] = before
    all_ref[...] = total


def along_y_kernel(chips, before_ref, all_ref, over_ref, mine_ref, other_ref, keep_ref, send_ref):
    at = lax.axis_index("seq")
    core = lax.rem(at, 2)
    y = lax.div(at, 2 * chips)
    before = before_ref[...] + jnp.where(y > 0, over_ref[...], 0.0)
    keep_ref[:, :DH] = before + jnp.where(core > 0, other_ref[...], 0.0)
    send_ref[:, :DH] = before + jnp.where(core > 0, 0.0, mine_ref[...])
    rows = keep_ref.shape[1] - DH
    partner = at + 1 - 2 * core
    for i in range(keep_ref.shape[0]):
        for ref, place in ((keep_ref, at), (send_ref, partner)):
            some = pl.ds(pl.multiple_of(place * rows, 8), rows)
            ref[i, DH:] = all_ref[i, some] + over_ref[i, some]


def inside_kernel(first, heads, block, q_ref, ka0_ref, va0_ref, ka1_ref, va1_ref, run_in, base_ref, qa_ref, run_ref):
    count = qa_ref.shape[0] // block
    half = heads // 2
    starts = [pair_start(q_ref.shape[1], own) for own in (True, False)]
    run_ref[...] = run_in[...]
    causal = lax.broadcasted_iota(jnp.int32, (block, block), 0) >= lax.broadcasted_iota(
        jnp.int32, (block, block), 1
    )

    @pl.loop(0, count, unroll=2)
    def _(n):
        part = pl.ds(pl.multiple_of(n * block, block), block)
        whole = pl.ds(pl.multiple_of((first + n) * block, block), block)
        for h in range(heads):
            ka_ref, va_ref = (ka0_ref, va0_ref) if h < half else (ka1_ref, va1_ref)
            i = h % half
            q = silu(q_ref[whole, pl.ds(pl.multiple_of(starts[h // half] + i * DH, DH), DH)])
            k = ka_ref[whole, cols_of(i)]
            v = va_ref[whole, cols_of(i)]
            scores = jnp.where(causal, dot(q, k, ((1,), (1,))), 0.0).astype(BF16)
            state = run_ref[h]
            hi = state.astype(BF16)
            lo = (state - hi.astype(F32)).astype(BF16)
            left = jnp.concatenate([scores, q, q], axis=1)
            right = jnp.concatenate([v, hi, lo], axis=0)
            base_ref[part, cols_of(h)] = dot(left, right, ((1,), (0,)))
            qa_ref[part, cols_of(h)] = q
            run_ref[h] = state + dot(k, v, ((0,), (0,)))


def gate_kernel(block, own_ref, rest_ref, gate_hbm, gain_ref, out_ref, gate_in, sems):
    count = gate_in.shape[0] // block
    width = gate_in.shape[1]

    def copy(n):
        part = pl.ds(n * block, block)
        return pltpu.make_async_copy(gate_hbm.at[part], gate_in.at[part], sems.at[n])

    for n in range(count):
        copy(n).start()
    places = [pl.ds(pair_start(width, own), width // 2) for own in (True, False)]

    @pl.loop(0, count)
    def _(n):
        copy(n).wait()
        part = pl.ds(pl.multiple_of(n * block, block), block)
        for attn_ref, cols in zip((own_ref, rest_ref), places):
            sigmoid = 0.5 + 0.5 * jnp.tanh(gate_in[part, cols].astype(F32) * 0.5)
            out_ref[part, cols] = attn_ref[part] * (gain_ref[:, cols] * sigmoid)


def carry(pair, block, base_refs, qa_refs, state_ref, attn_ref, states, finish):
    half = state_ref.shape[0]
    for i in range(half):
        state = state_ref[i, :DH]
        hi = state.astype(BF16)
        states[i, :DH] = hi
        states[i, DH:] = (state - hi.astype(F32)).astype(BF16)
    first = 0
    for base_ref, qa_ref in zip(base_refs, qa_refs):

        @pl.loop(0, base_ref.shape[0] // block, unroll=2)
        def _(n):
            part = pl.ds(pl.multiple_of(n * block, block), block)
            whole = pl.ds(pl.multiple_of((first + n) * block, block), block)
            sums = None
            for i in range(half):
                wide = cols_of(pair * half + i)
                q = qa_ref[part, wide]
                attn = base_ref[part, wide] + dot(
                    jnp.concatenate([q, q], axis=1), states[i], ((1,), (0,))
                )
                attn_ref[whole, cols_of(i)] = attn
                sums = attn * attn if sums is None else sums + attn * attn
            finish(whole, sums)

        first += base_ref.shape[0] // block


def carry_own_kernel(
    block, base0_ref, base1_ref, qa0_ref, qa1_ref, keep_ref, attn_ref, sums_ref, states
):
    def finish(whole, sums):
        sums_ref[whole] = sums

    carry(0, block, (base0_ref, base1_ref), (qa0_ref, qa1_ref), keep_ref, attn_ref, states, finish)


def carry_rest_kernel(
    block, base0_ref, base1_ref, qa0_ref, qa1_ref, keep_ref, got_ref, sums_ref,
    attn_ref, mine_ref, states, squares,
):
    def finish(whole, sums):
        sums = sums + sums_ref[whole]
        hi = sums.astype(BF16)
        squares[whole, :DH] = hi
        squares[whole, DH:] = (sums - hi.astype(F32)).astype(BF16)

    carry(1, block, (base0_ref, base1_ref), (qa0_ref, qa1_ref), got_ref, attn_ref, states, finish)
    across = dot(jnp.ones((16, 2 * DH), BF16), squares[...], ((1,), (1,)))
    token_rows = squares.shape[0] // DH
    for c in range(token_rows):
        mine_ref[c : c + 1] = across[:1, cols_of(c)]
    core = lax.rem(lax.axis_index("seq"), 2)
    half, rows = keep_ref.shape[0], keep_ref.shape[1] - DH
    for i in range(half):
        for ref, h in ((keep_ref, core * half + i), (got_ref, (1 - core) * half + i)):
            mine_ref[pl.ds(pl.multiple_of(token_rows + h * rows, 8), rows)] = ref[i, DH:]


def pack_kernel(owners_ref, mine_ref, other_ref, send_ref):
    side = lax.rem(lax.axis_index("grp"), 2)
    rows = owners_ref.shape[1]
    width = mine_ref.shape[0]
    token_rows = width - 4 * rows
    own, other = owners_ref[0] - side, owners_ref[1] - side
    both = mine_ref[:token_rows] + other_ref[:token_rows]
    for place, g in enumerate(lines(2 * send_ref.shape[0])[0]):
        send_ref[place, :token_rows] = both
        for at in range(token_rows, width, rows):
            part = slice(at, at + rows)
            send_ref[place, part] = jnp.where(
                own == g, mine_ref[part], jnp.where(other == g, other_ref[part], 0.0)
            )


def norm_kernel(heads, features, block, got_ref, gated_ref, out_hbm, state_ref, out, scales, sems):
    total = got_ref[0]
    for place in range(1, got_ref.shape[0]):
        total = total + got_ref[place]
    rows = state_ref.shape[1]
    tokens = out.shape[0]
    token_rows = tokens // DH
    scales[...] = jnp.zeros_like(scales)
    scales[:token_rows] = lax.rsqrt(total[:token_rows] / features + 1e-6)
    columns = jnp.transpose(scales[...])
    copies = []
    for n in range(tokens // block):
        for c in range(n * block // DH, (n + 1) * block // DH):
            part = slice(c * DH, (c + 1) * DH)
            out[part] = (gated_ref[part] * columns[:, c : c + 1]).astype(BF16)
        part = pl.ds(n * block, block)
        copies.append(pltpu.make_async_copy(out.at[part], out_hbm.at[part], sems.at[n]))
        copies[-1].start()
    for h in range(heads):
        at = token_rows + h * rows
        state_ref[h] = total[at : at + rows]
    for copy in copies:
        copy.wait()


def body(query_in, key_in, value_in, gate_in, norm_gain, head_owner):
    tokens, width = query_in.shape
    heads = width // DH
    half = heads // 2
    shards = lax.axis_size("seq")
    groups = lax.axis_size("grp")
    chips = 4
    block = min(256, tokens)
    count = tokens // block
    chunk = 2 * block
    rows = DH // shards
    token_rows = tokens // DH
    wide = pltpu.VMEM((tokens, width), BF16)
    pair_state = pltpu.VMEM((half, DH, DH), F32)
    dma = lambda *shape: pltpu.SemaphoreType.DMA(shape)
    limit = params(24)

    half_wide = pltpu.VMEM((tokens, half * DH), BF16)
    k_in, v_in, query, ka1, va1, give = pl.pallas_call(
        functools.partial(give_kernel, chunk),
        in_specs=[HBM] * 3,
        out_specs=[VMEM] * 6,
        out_shape=[wide] * 3 + [half_wide] * 2 + [pair_state],
        scratch_shapes=[dma(2, tokens // chunk), pltpu.SemaphoreType.DMA],
        compiler_params=limit,
        cost_estimate=cost(tokens * width * DH, 6 * tokens * width),
        name="give",
    )(in_hbm(key_in), in_hbm(value_in), in_hbm(query_in))

    def swap(x, bit):
        return lax.ppermute(x, "seq", [(i, i ^ bit) for i in range(shards)])

    def on_x(x, k):
        place = lambda i: i - i % (2 * chips) + (i + 2 * k) % (2 * chips)
        return lax.ppermute(x, "seq", [(i, place(i)) for i in range(shards)])

    def inside(first, blocks, q, acts, run):
        part = blocks * block
        return pl.pallas_call(
            functools.partial(inside_kernel, first, heads, block),
            in_specs=[VMEM] * 6,
            out_specs=[VMEM] * 3,
            out_shape=[
                pltpu.VMEM((part, width), F32),
                pltpu.VMEM((part, width), BF16),
                pltpu.VMEM((heads, DH, DH), F32),
            ],
            compiler_params=limit,
            cost_estimate=cost(2 * part * width * (2 * block + 3 * DH), 12 * part * width),
            name="inside%d" % first,
        )(q, *acts, run)

    cut = 5 * count // 8
    other = swap(give, 1)
    k_in, _ = lax.optimization_barrier((k_in, give))
    ka0, va0, mine, owners = pl.pallas_call(
        functools.partial(mine_kernel, chunk),
        in_specs=[VMEM, VMEM, HBM],
        out_specs=[VMEM] * 4,
        out_shape=[half_wide] * 2 + [pair_state, pltpu.VMEM((2, rows, DH), jnp.int32)],
        scratch_shapes=[pltpu.SMEM(head_owner.shape, jnp.int32), pltpu.SemaphoreType.DMA],
        compiler_params=limit,
        cost_estimate=cost(tokens * width * DH, 3 * tokens * width),
        name="mine",
    )(k_in, v_in, in_hbm(head_owner))
    other, mine = lax.optimization_barrier((other, mine))
    pair = pl.pallas_call(
        pair_kernel, in_specs=[VMEM] * 2, out_specs=VMEM, out_shape=pair_state,
        compiler_params=limit, name="pair",
    )(mine, other)
    around = [on_x(pair, k) for k in range(chips - 1, 0, -1)]
    acts = lax.optimization_barrier((ka0, va0, ka1, va1, pair))[:4]
    base0, qa0, run = inside(0, cut, query, acts, jnp.zeros((heads, DH, DH), F32))
    base0, *around = lax.optimization_barrier((base0, *around))
    before_x, all_x = pl.pallas_call(
        functools.partial(along_x_kernel, chips),
        in_specs=[VMEM] * chips, out_specs=[VMEM] * 2, out_shape=[pair_state] * 2,
        compiler_params=limit, name="along_x",
    )(pair, *around)
    over = swap(all_x, 2 * chips)
    run, _ = lax.optimization_barrier((run, all_x))
    base1, qa1, _ = inside(cut, count - cut, query, acts, run)
    base1, over = lax.optimization_barrier((base1, over))
    keep, send_core = pl.pallas_call(
        functools.partial(along_y_kernel, chips),
        in_specs=[VMEM] * 5, out_specs=[VMEM] * 2,
        out_shape=[pltpu.VMEM((half, DH + rows, DH), F32)] * 2,
        compiler_params=limit, name="along_y",
    )(before_x, all_x, over, mine, other)
    got_core = swap(send_core, 1)
    payload = token_rows + heads * rows
    half_attn = pltpu.VMEM((tokens, half * DH), F32)
    states = pltpu.VMEM((half, 2 * DH, DH), BF16)
    attn_own, sums = pl.pallas_call(
        functools.partial(carry_own_kernel, block),
        in_specs=[VMEM] * 5,
        out_specs=[VMEM] * 2,
        out_shape=[half_attn, pltpu.VMEM((tokens, DH), F32)],
        scratch_shapes=[states],
        compiler_params=limit,
        cost_estimate=cost(2 * tokens * width * DH, 5 * tokens * width),
        name="carry_own",
    )(base0, base1, qa0, qa1, keep)
    sums, got_core = lax.optimization_barrier((sums, got_core))
    attn_rest, own = pl.pallas_call(
        functools.partial(carry_rest_kernel, block),
        in_specs=[VMEM] * 7,
        out_specs=[VMEM] * 2,
        out_shape=[half_attn, pltpu.VMEM((payload, DH), F32)],
        scratch_shapes=[states, pltpu.VMEM((tokens, 2 * DH), BF16)],
        compiler_params=limit,
        cost_estimate=cost(2 * tokens * width * DH, 5 * tokens * width),
        name="carry_rest",
    )(base0, base1, qa0, qa1, keep, got_core, sums)

    beside = lax.ppermute(own, "grp", [(g, g ^ 1) for g in range(groups)])
    gated = pl.pallas_call(
        functools.partial(gate_kernel, block),
        in_specs=[VMEM, VMEM, HBM, VMEM],
        out_specs=VMEM,
        out_shape=pltpu.VMEM((tokens, width), F32),
        scratch_shapes=[pltpu.VMEM((tokens, width), BF16), dma(count)],
        compiler_params=limit,
        cost_estimate=cost(4 * tokens * width, 10 * tokens * width),
        name="gate",
    )(attn_own, attn_rest, in_hbm(gate_in), norm_gain.reshape(1, width))
    gated, beside = lax.optimization_barrier((gated, beside))
    send = pl.pallas_call(
        pack_kernel,
        in_specs=[VMEM] * 3,
        out_specs=VMEM,
        out_shape=pltpu.VMEM((groups // 2, payload, DH), F32),
        compiler_params=limit,
        name="pack",
    )(owners, own, beside)

    got = lax.all_to_all(
        send, "grp", 0, 0, tiled=True, axis_index_groups=lines(groups)
    )

    attn_out, decode_state = pl.pallas_call(
        functools.partial(norm_kernel, heads, float(width * groups), block),
        in_specs=[VMEM, VMEM],
        out_specs=[HBM, VMEM],
        out_shape=[
            jax.ShapeDtypeStruct((tokens, width), BF16),
            jax.ShapeDtypeStruct((heads, rows, DH), F32),
        ],
        scratch_shapes=[
            pltpu.VMEM((tokens, width), BF16),
            pltpu.VMEM((DH, DH), F32),
            dma(count),
        ],
        compiler_params=limit,
        cost_estimate=cost(2 * tokens * width, 6 * tokens * width),
        name="norm",
    )(got, gated)
    return attn_out, decode_state


def solution(mesh):
    return jax.shard_map(
        body,
        mesh=mesh,
        in_specs=(
            P("seq", "grp"),
            P("seq", "grp"),
            P("seq", "grp"),
            P("seq", "grp"),
            P("grp"),
            P(),
        ),
        out_specs=(P("seq", "grp"), P("grp", "seq", None)),
        check_vma=False,
    )
```

```python
import functools

import jax
import jax.numpy as jnp
from jax import lax
from jax.experimental import pallas as pl
from jax.experimental.pallas import tpu as pltpu
from jax.sharding import PartitionSpec as P

DH = 128
HOPS = (2, 3, 1)
F32 = jnp.float32
BF16 = jnp.bfloat16
MIB = 1 << 20
VMEM = pl.BlockSpec(memory_space=pltpu.VMEM)
HBM = pl.BlockSpec(memory_space=pltpu.HBM)


def lines(groups):
    count = groups // 2
    order = [6, 5, 4, 7, 3, 2, 1, 0] if count == 8 else list(range(count))[::-1]
    return [[2 * at + side for at in order] for side in range(2)]


def dot(a, b, dims):
    return lax.dot_general(a, b, (dims, ((), ())), preferred_element_type=F32)


def silu(x):
    half = x.astype(F32) * 0.5
    return (half + half * jnp.tanh(half)).astype(BF16)


def params(mib):
    return pltpu.CompilerParams(vmem_limit_bytes=mib * MIB)


def cost(flops, nbytes, trans=0):
    return pl.CostEstimate(flops=flops, bytes_accessed=nbytes, transcendentals=trans)


def in_hbm(x):
    return pltpu.with_memory_space_constraint(x, pltpu.HBM)


def cols_of(h):
    return slice(h * DH, (h + 1) * DH)


def pair_start(width, own):
    core = lax.rem(lax.axis_index("seq"), 2)
    return pl.multiple_of((core if own else 1 - core) * (width // 2), width // 2)


def add_states(first, c, part, k_in, v_in, ka_ref, va_ref, state_ref, runs_ref):
    runs_ref[c] = state_ref[...]
    for i in range(state_ref.shape[0]):
        wide = pl.ds(pl.multiple_of(first + i * DH, DH), DH)
        k = silu(k_in[part, wide])
        v = silu(v_in[part, wide])
        ka_ref[part, cols_of(i)] = k
        va_ref[part, cols_of(i)] = v
        state_ref[i] += dot(k, v, ((0,), (0,)))


def give_kernel(
    chunk, k_hbm, v_hbm, k_in, v_in, ka_ref, va_ref, give_ref, runs_ref, sems, late
):
    tokens, width = k_in.shape
    count = tokens // chunk
    first = pair_start(width, False)

    def pair(c):
        place = (pl.ds(c * chunk, chunk), pl.ds(first, width // 2))
        return [
            pltpu.make_async_copy(k_hbm.at[place], k_in.at[place], sems.at[0, c]),
            pltpu.make_async_copy(v_hbm.at[place], v_in.at[place], sems.at[1, c]),
        ]

    own = (slice(None), pl.ds(pair_start(width, True), width // 2))
    later = [
        pltpu.make_async_copy(k_hbm.at[own], k_in.at[own], late.at[0]),
        pltpu.make_async_copy(v_hbm.at[own], v_in.at[own], late.at[1]),
    ]
    for c in range(count):
        for copy in pair(c):
            copy.start()
    for copy in later:
        copy.start()
    give_ref[...] = jnp.zeros_like(give_ref)

    @pl.loop(0, count)
    def _(c):
        for copy in pair(c):
            copy.wait()
        part = pl.ds(pl.multiple_of(c * chunk, chunk), chunk)
        add_states(first, c, part, k_in, v_in, ka_ref, va_ref, give_ref, runs_ref)

    for copy in later:
        copy.wait()


def mine_kernel(
    chunk, k_in, v_in, q_hbm, owner_hbm, ka_ref, va_ref, mine_ref, runs_ref, q_ref, owners_ref, owner, sems
):
    copies = [
        pltpu.make_async_copy(q_hbm, q_ref, sems.at[0]),
        pltpu.make_async_copy(owner_hbm, owner, sems.at[1]),
    ]
    for copy in copies:
        copy.start()
    mine_ref[...] = jnp.zeros_like(mine_ref)
    first = pair_start(k_in.shape[1], True)

    @pl.loop(0, k_in.shape[0] // chunk)
    def _(c):
        part = pl.ds(pl.multiple_of(c * chunk, chunk), chunk)
        add_states(first, c, part, k_in, v_in, ka_ref, va_ref, mine_ref, runs_ref)

    for copy in copies:
        copy.wait()
    group = lax.axis_index("grp")
    for at, g in enumerate((group, group + 1 - 2 * lax.rem(group, 2))):
        owners_ref[at] = jnp.full(owners_ref.shape[1:], owner[g], jnp.int32)


def pair_kernel(mine_ref, other_ref, out_ref):
    out_ref[...] = mine_ref[...] + other_ref[...]


def along_x_kernel(chips, own_ref, *refs):
    got, (before_ref, all_ref) = refs[: chips - 1], refs[chips - 1 :]
    x = lax.rem(lax.div(lax.axis_index("seq"), 2), chips)
    total = own_ref[...]
    before = jnp.zeros_like(total)
    for back in range(1, chips):
        part = got[HOPS.index(back)][...]
        total = total + part
        before = before + jnp.where(x >= back, part, 0.0)
    before_ref[...] = before
    all_ref[...] = total


def along_y_kernel(chips, before_ref, all_ref, over_ref, mine_ref, other_ref, keep_ref, send_ref):
    at = lax.axis_index("seq")
    core = lax.rem(at, 2)
    y = lax.div(at, 2 * chips)
    before = before_ref[...] + jnp.where(y > 0, over_ref[...], 0.0)
    keep_ref[:, :DH] = before + jnp.where(core > 0, other_ref[...], 0.0)
    send_ref[:, :DH] = before + jnp.where(core > 0, 0.0, mine_ref[...])
    rows = keep_ref.shape[1] - DH
    partner = at + 1 - 2 * core
    for i in range(keep_ref.shape[0]):
        for ref, place in ((keep_ref, at), (send_ref, partner)):
            some = pl.ds(pl.multiple_of(place * rows, 8), rows)
            ref[i, DH:] = all_ref[i, some] + over_ref[i, some]


def inside_kernel(
    first, heads, block, q_ref, ka0_ref, va0_ref, runs0_ref, ka1_ref, va1_ref, runs1_ref,
    base_ref, qa_ref,
):
    count = qa_ref.shape[0] // block
    half = heads // 2
    starts = [pair_start(q_ref.shape[1], own) for own in (True, False)]
    causal = (
        lax.broadcasted_iota(jnp.int32, (block, block), 0)
        >= lax.broadcasted_iota(jnp.int32, (block, block), 1)
    ).astype(BF16)

    @pl.loop(0, count // 2)
    def _(c):
        for h in range(heads):
            ka_ref, va_ref, runs_ref = (
                (ka0_ref, va0_ref, runs0_ref) if h < half else (ka1_ref, va1_ref, runs1_ref)
            )
            i = h % half
            column = pl.ds(pl.multiple_of(starts[h // half] + i * DH, DH), DH)
            state = runs_ref[first // 2 + c, i]
            for odd in range(2):
                part = pl.ds(pl.multiple_of((2 * c + odd) * block, block), block)
                whole = pl.ds(pl.multiple_of((first + 2 * c + odd) * block, block), block)
                q = silu(q_ref[whole, column])
                k = ka_ref[whole, cols_of(i)]
                v = va_ref[whole, cols_of(i)]
                scores = dot(q, k, ((1,), (1,))).astype(BF16) * causal
                hi = state.astype(BF16)
                lo = (state - hi.astype(F32)).astype(BF16)
                left = jnp.concatenate([scores, q, q], axis=1)
                right = jnp.concatenate([v, hi, lo], axis=0)
                base_ref[part, cols_of(h)] = dot(left, right, ((1,), (0,)))
                qa_ref[part, cols_of(h)] = q
                if not odd:
                    state = state + dot(k, v, ((0,), (0,)))


def gate_kernel(block, own_ref, rest_ref, gate_hbm, gain_ref, out_ref, gate_in, sems):
    count = gate_in.shape[0] // block
    width = gate_in.shape[1]

    def copy(n):
        part = pl.ds(n * block, block)
        return pltpu.make_async_copy(gate_hbm.at[part], gate_in.at[part], sems.at[n])

    for n in range(count):
        copy(n).start()
    places = [pl.ds(pair_start(width, own), width // 2) for own in (True, False)]

    @pl.loop(0, count)
    def _(n):
        copy(n).wait()
        part = pl.ds(pl.multiple_of(n * block, block), block)
        for attn_ref, cols in zip((own_ref, rest_ref), places):
            sigmoid = 0.5 + 0.5 * jnp.tanh(gate_in[part, cols].astype(F32) * 0.5)
            out_ref[part, cols] = attn_ref[part] * (gain_ref[:, cols] * sigmoid)


def carry(pair, block, base_refs, qa_refs, state_ref, attn_ref, states, finish):
    half = state_ref.shape[0]
    for i in range(half):
        state = state_ref[i, :DH]
        hi = state.astype(BF16)
        states[i, :DH] = hi
        states[i, DH:] = (state - hi.astype(F32)).astype(BF16)
    first = 0
    for base_ref, qa_ref in zip(base_refs, qa_refs):

        @pl.loop(0, base_ref.shape[0] // block, unroll=True)
        def _(n):
            part = pl.ds(pl.multiple_of(n * block, block), block)
            whole = pl.ds(pl.multiple_of((first + n) * block, block), block)
            sums = None
            for i in range(half):
                wide = cols_of(pair * half + i)
                q = qa_ref[part, wide]
                attn = base_ref[part, wide] + dot(
                    jnp.concatenate([q, q], axis=1), states[i], ((1,), (0,))
                )
                attn_ref[whole, cols_of(i)] = attn
                sums = attn * attn if sums is None else sums + attn * attn
            finish(whole, sums)

        first += base_ref.shape[0] // block


def carry_own_kernel(
    block, base0_ref, base1_ref, qa0_ref, qa1_ref, keep_ref, attn_ref, sums_ref, states
):
    def finish(whole, sums):
        sums_ref[whole] = sums

    carry(0, block, (base0_ref, base1_ref), (qa0_ref, qa1_ref), keep_ref, attn_ref, states, finish)


def carry_rest_kernel(
    block, base0_ref, base1_ref, qa0_ref, qa1_ref, keep_ref, got_ref, sums_ref,
    attn_ref, mine_ref, states, squares,
):
    def finish(whole, sums):
        sums = sums + sums_ref[whole]
        hi = sums.astype(BF16)
        squares[whole, :DH] = hi
        squares[whole, DH:] = (sums - hi.astype(F32)).astype(BF16)

    carry(1, block, (base0_ref, base1_ref), (qa0_ref, qa1_ref), got_ref, attn_ref, states, finish)
    across = dot(jnp.ones((16, 2 * DH), BF16), squares[...], ((1,), (1,)))
    token_rows = squares.shape[0] // DH
    for c in range(token_rows):
        mine_ref[c : c + 1] = across[:1, cols_of(c)]
    core = lax.rem(lax.axis_index("seq"), 2)
    half, rows = keep_ref.shape[0], keep_ref.shape[1] - DH
    for i in range(half):
        for ref, h in ((keep_ref, core * half + i), (got_ref, (1 - core) * half + i)):
            mine_ref[pl.ds(pl.multiple_of(token_rows + h * rows, 8), rows)] = ref[i, DH:]


def pack_kernel(owners_ref, mine_ref, other_ref, send_ref):
    side = lax.rem(lax.axis_index("grp"), 2)
    rows = owners_ref.shape[1]
    width = mine_ref.shape[0]
    token_rows = width - 4 * rows
    own, other = owners_ref[0] - side, owners_ref[1] - side
    both = mine_ref[:token_rows] + other_ref[:token_rows]
    for place, g in enumerate(lines(2 * send_ref.shape[0])[0]):
        send_ref[place, :token_rows] = both
        for at in range(token_rows, width, rows):
            part = slice(at, at + rows)
            send_ref[place, part] = jnp.where(
                own == g, mine_ref[part], jnp.where(other == g, other_ref[part], 0.0)
            )


def norm_kernel(heads, features, block, got_ref, gated_ref, out_hbm, state_ref, out, scales, sems):
    total = got_ref[0]
    for place in range(1, got_ref.shape[0]):
        total = total + got_ref[place]
    rows = state_ref.shape[1]
    tokens = out.shape[0]
    token_rows = tokens // DH
    scales[...] = jnp.zeros_like(scales)
    scales[:token_rows] = lax.rsqrt(total[:token_rows] / features + 1e-6)
    columns = jnp.transpose(scales[...])
    copies = []
    for n in range(tokens // block):
        for c in range(n * block // DH, (n + 1) * block // DH):
            part = slice(c * DH, (c + 1) * DH)
            out[part] = (gated_ref[part] * columns[:, c : c + 1]).astype(BF16)
        part = pl.ds(n * block, block)
        copies.append(pltpu.make_async_copy(out.at[part], out_hbm.at[part], sems.at[n]))
        copies[-1].start()
    for h in range(heads):
        at = token_rows + h * rows
        state_ref[h] = total[at : at + rows]
    for copy in copies:
        copy.wait()


def body(query_in, key_in, value_in, gate_in, norm_gain, head_owner):
    tokens, width = query_in.shape
    heads = width // DH
    half = heads // 2
    shards = lax.axis_size("seq")
    groups = lax.axis_size("grp")
    chips = 4
    block = min(256, tokens)
    count = tokens // block
    chunk = 2 * block
    rows = DH // shards
    token_rows = tokens // DH
    wide = pltpu.VMEM((tokens, width), BF16)
    pair_state = pltpu.VMEM((half, DH, DH), F32)
    dma = lambda *shape: pltpu.SemaphoreType.DMA(shape)
    limit = params(24)

    half_wide = pltpu.VMEM((tokens, half * DH), BF16)
    runs = pltpu.VMEM((tokens // chunk, half, DH, DH), F32)
    k_in, v_in, ka1, va1, give, runs1 = pl.pallas_call(
        functools.partial(give_kernel, chunk),
        in_specs=[HBM] * 2,
        out_specs=[VMEM] * 6,
        out_shape=[wide] * 2 + [half_wide] * 2 + [pair_state, runs],
        scratch_shapes=[dma(2, tokens // chunk), dma(2)],
        compiler_params=limit,
        cost_estimate=cost(tokens * width * DH, 6 * tokens * width),
        name="give",
    )(in_hbm(key_in), in_hbm(value_in))

    def swap(x, bit):
        return lax.ppermute(x, "seq", [(i, i ^ bit) for i in range(shards)])

    def on_x(x, k):
        place = lambda i: i - i % (2 * chips) + (i + 2 * k) % (2 * chips)
        return lax.ppermute(x, "seq", [(i, place(i)) for i in range(shards)])

    def inside(first, blocks, q, acts):
        part = blocks * block
        return pl.pallas_call(
            functools.partial(inside_kernel, first, heads, block),
            in_specs=[VMEM] * 7,
            out_specs=[VMEM] * 2,
            out_shape=[
                pltpu.VMEM((part, width), F32),
                pltpu.VMEM((part, width), BF16),
            ],
            compiler_params=limit,
            cost_estimate=cost(2 * part * width * (2 * block + 3 * DH), 12 * part * width),
            name="inside%d" % first,
        )(q, *acts)

    cut = 6 * count // 8
    other = swap(give, 1)
    k_in, _ = lax.optimization_barrier((k_in, give))
    ka0, va0, mine, runs0, query, owners = pl.pallas_call(
        functools.partial(mine_kernel, chunk),
        in_specs=[VMEM, VMEM, HBM, HBM],
        out_specs=[VMEM] * 6,
        out_shape=[half_wide] * 2
        + [pair_state, runs, wide, pltpu.VMEM((2, rows, DH), jnp.int32)],
        scratch_shapes=[pltpu.SMEM(head_owner.shape, jnp.int32), dma(2)],
        compiler_params=limit,
        cost_estimate=cost(tokens * width * DH, 3 * tokens * width),
        name="mine",
    )(k_in, v_in, in_hbm(query_in), in_hbm(head_owner))
    other, mine = lax.optimization_barrier((other, mine))
    pair = pl.pallas_call(
        pair_kernel, in_specs=[VMEM] * 2, out_specs=VMEM, out_shape=pair_state,
        compiler_params=limit, name="pair",
    )(mine, other)
    around = [on_x(pair, k) for k in HOPS]
    acts = lax.optimization_barrier((ka0, va0, runs0, ka1, va1, runs1, pair))[:6]
    base0, qa0 = inside(0, cut, query, acts)
    base0, *around = lax.optimization_barrier((base0, *around))
    before_x, all_x = pl.pallas_call(
        functools.partial(along_x_kernel, chips),
        in_specs=[VMEM] * chips, out_specs=[VMEM] * 2, out_shape=[pair_state] * 2,
        compiler_params=limit, name="along_x",
    )(pair, *around)
    over = swap(all_x, 2 * chips)
    acts = lax.optimization_barrier((*acts, all_x))[:6]
    base1, qa1 = inside(cut, count - cut, query, acts)
    base1, over = lax.optimization_barrier((base1, over))
    keep, send_core = pl.pallas_call(
        functools.partial(along_y_kernel, chips),
        in_specs=[VMEM] * 5, out_specs=[VMEM] * 2,
        out_shape=[pltpu.VMEM((half, DH + rows, DH), F32)] * 2,
        compiler_params=limit, name="along_y",
    )(before_x, all_x, over, mine, other)
    got_core = swap(send_core, 1)
    payload = token_rows + heads * rows
    half_attn = pltpu.VMEM((tokens, half * DH), F32)
    states = pltpu.VMEM((half, 2 * DH, DH), BF16)
    attn_own, sums = pl.pallas_call(
        functools.partial(carry_own_kernel, block),
        in_specs=[VMEM] * 5,
        out_specs=[VMEM] * 2,
        out_shape=[half_attn, pltpu.VMEM((tokens, DH), F32)],
        scratch_shapes=[states],
        compiler_params=limit,
        cost_estimate=cost(2 * tokens * width * DH, 5 * tokens * width),
        name="carry_own",
    )(base0, base1, qa0, qa1, keep)
    sums, got_core = lax.optimization_barrier((sums, got_core))
    attn_rest, own = pl.pallas_call(
        functools.partial(carry_rest_kernel, block),
        in_specs=[VMEM] * 7,
        out_specs=[VMEM] * 2,
        out_shape=[half_attn, pltpu.VMEM((payload, DH), F32)],
        scratch_shapes=[states, pltpu.VMEM((tokens, 2 * DH), BF16)],
        compiler_params=limit,
        cost_estimate=cost(2 * tokens * width * DH, 5 * tokens * width),
        name="carry_rest",
    )(base0, base1, qa0, qa1, keep, got_core, sums)

    beside = lax.ppermute(own, "grp", [(g, g ^ 1) for g in range(groups)])
    gated = pl.pallas_call(
        functools.partial(gate_kernel, block),
        in_specs=[VMEM, VMEM, HBM, VMEM],
        out_specs=VMEM,
        out_shape=pltpu.VMEM((tokens, width), F32),
        scratch_shapes=[pltpu.VMEM((tokens, width), BF16), dma(count)],
        compiler_params=limit,
        cost_estimate=cost(4 * tokens * width, 10 * tokens * width),
        name="gate",
    )(attn_own, attn_rest, in_hbm(gate_in), norm_gain.reshape(1, width))
    gated, beside = lax.optimization_barrier((gated, beside))
    send = pl.pallas_call(
        pack_kernel,
        in_specs=[VMEM] * 3,
        out_specs=VMEM,
        out_shape=pltpu.VMEM((groups // 2, payload, DH), F32),
        compiler_params=limit,
        name="pack",
    )(owners, own, beside)

    got = lax.all_to_all(
        send, "grp", 0, 0, tiled=True, axis_index_groups=lines(groups)
    )

    attn_out, decode_state = pl.pallas_call(
        functools.partial(norm_kernel, heads, float(width * groups), block),
        in_specs=[VMEM, VMEM],
        out_specs=[HBM, VMEM],
        out_shape=[
            jax.ShapeDtypeStruct((tokens, width), BF16),
            jax.ShapeDtypeStruct((heads, rows, DH), F32),
        ],
        scratch_shapes=[
            pltpu.VMEM((tokens, width), BF16),
            pltpu.VMEM((DH, DH), F32),
            dma(count),
        ],
        compiler_params=limit,
        cost_estimate=cost(2 * tokens * width, 6 * tokens * width),
        name="norm",
    )(got, gated)
    return attn_out, decode_state


def solution(mesh):
    return jax.shard_map(
        body,
        mesh=mesh,
        in_specs=(
            P("seq", "grp"),
            P("seq", "grp"),
            P("seq", "grp"),
            P("seq", "grp"),
            P("grp"),
            P(),
        ),
        out_specs=(P("seq", "grp"), P("grp", "seq", None)),
        check_vma=False,
    )
```

```python
import functools

import jax
import jax.numpy as jnp
from jax import lax
from jax.experimental import pallas as pl
from jax.experimental.pallas import tpu as pltpu
from jax.sharding import PartitionSpec as P

DH = 128
HOPS = (2, 3, 1)
F32 = jnp.float32
BF16 = jnp.bfloat16
MIB = 1 << 20
VMEM = pl.BlockSpec(memory_space=pltpu.VMEM)
HBM = pl.BlockSpec(memory_space=pltpu.HBM)


def lines(groups):
    count = groups // 2
    order = [6, 5, 4, 7, 3, 2, 1, 0] if count == 8 else list(range(count))[::-1]
    return [[2 * at + side for at in order] for side in range(2)]


def dot(a, b, dims):
    return lax.dot_general(a, b, (dims, ((), ())), preferred_element_type=F32)


def silu(x):
    half = x.astype(F32) * 0.5
    return (half + half * jnp.tanh(half)).astype(BF16)


def params(mib):
    return pltpu.CompilerParams(vmem_limit_bytes=mib * MIB)


def cost(flops, nbytes, trans=0):
    return pl.CostEstimate(flops=flops, bytes_accessed=nbytes, transcendentals=trans)


def in_hbm(x):
    return pltpu.with_memory_space_constraint(x, pltpu.HBM)


def cols_of(h):
    return slice(h * DH, (h + 1) * DH)


def pair_start(width, own):
    core = lax.rem(lax.axis_index("seq"), 2)
    return pl.multiple_of((core if own else 1 - core) * (width // 2), width // 2)


def add_states(first, c, part, k_in, v_in, ka_ref, va_ref, state_ref, runs_ref):
    runs_ref[c] = state_ref[...]
    for i in range(state_ref.shape[0]):
        wide = pl.ds(pl.multiple_of(first + i * DH, DH), DH)
        k = silu(k_in[part, wide])
        v = silu(v_in[part, wide])
        ka_ref[part, cols_of(i)] = k
        va_ref[part, cols_of(i)] = v
        state_ref[i] += dot(k, v, ((0,), (0,)))


def give_kernel(
    chunk, k_hbm, v_hbm, k_in, v_in, ka_ref, va_ref, give_ref, runs_ref, sems, late
):
    tokens, width = k_in.shape
    count = tokens // chunk
    first = pair_start(width, False)

    def pair(c):
        place = (pl.ds(c * chunk, chunk), pl.ds(first, width // 2))
        return [
            pltpu.make_async_copy(k_hbm.at[place], k_in.at[place], sems.at[0, c]),
            pltpu.make_async_copy(v_hbm.at[place], v_in.at[place], sems.at[1, c]),
        ]

    own = (slice(None), pl.ds(pair_start(width, True), width // 2))
    later = [
        pltpu.make_async_copy(k_hbm.at[own], k_in.at[own], late.at[0]),
        pltpu.make_async_copy(v_hbm.at[own], v_in.at[own], late.at[1]),
    ]
    for c in range(count):
        for copy in pair(c):
            copy.start()
    for copy in later:
        copy.start()
    give_ref[...] = jnp.zeros_like(give_ref)

    @pl.loop(0, count)
    def _(c):
        for copy in pair(c):
            copy.wait()
        part = pl.ds(pl.multiple_of(c * chunk, chunk), chunk)
        add_states(first, c, part, k_in, v_in, ka_ref, va_ref, give_ref, runs_ref)

    for copy in later:
        copy.wait()


def mine_kernel(
    chunk, k_in, v_in, q_hbm, owner_hbm, ka_ref, va_ref, mine_ref, runs_ref, q_ref, owners_ref, owner, sems
):
    copies = [
        pltpu.make_async_copy(q_hbm, q_ref, sems.at[0]),
        pltpu.make_async_copy(owner_hbm, owner, sems.at[1]),
    ]
    for copy in copies:
        copy.start()
    mine_ref[...] = jnp.zeros_like(mine_ref)
    first = pair_start(k_in.shape[1], True)

    @pl.loop(0, k_in.shape[0] // chunk)
    def _(c):
        part = pl.ds(pl.multiple_of(c * chunk, chunk), chunk)
        add_states(first, c, part, k_in, v_in, ka_ref, va_ref, mine_ref, runs_ref)

    for copy in copies:
        copy.wait()
    group = lax.axis_index("grp")
    for at, g in enumerate((group, group + 1 - 2 * lax.rem(group, 2))):
        owners_ref[at] = jnp.full(owners_ref.shape[1:], owner[g], jnp.int32)


def pair_kernel(mine_ref, other_ref, out_ref):
    out_ref[...] = mine_ref[...] + other_ref[...]


def along_x_kernel(chips, own_ref, *refs):
    got, (before_ref, all_ref) = refs[: chips - 1], refs[chips - 1 :]
    x = lax.rem(lax.div(lax.axis_index("seq"), 2), chips)
    total = own_ref[...]
    before = jnp.zeros_like(total)
    for back in range(1, chips):
        part = got[HOPS.index(back)][...]
        total = total + part
        before = before + jnp.where(x >= back, part, 0.0)
    before_ref[...] = before
    all_ref[...] = total


def along_y_kernel(chips, before_ref, all_ref, over_ref, mine_ref, other_ref, keep_ref, send_ref):
    at = lax.axis_index("seq")
    core = lax.rem(at, 2)
    y = lax.div(at, 2 * chips)
    before = before_ref[...] + jnp.where(y > 0, over_ref[...], 0.0)
    keep_ref[:, :DH] = before + jnp.where(core > 0, other_ref[...], 0.0)
    send_ref[:, :DH] = before + jnp.where(core > 0, 0.0, mine_ref[...])
    rows = keep_ref.shape[1] - DH
    partner = at + 1 - 2 * core
    for i in range(keep_ref.shape[0]):
        for ref, place in ((keep_ref, at), (send_ref, partner)):
            some = pl.ds(pl.multiple_of(place * rows, 8), rows)
            ref[i, DH:] = all_ref[i, some] + over_ref[i, some]


def inside_kernel(
    first, heads, block, q_ref, ka0_ref, va0_ref, runs0_ref, ka1_ref, va1_ref, runs1_ref,
    base_ref, qa_ref,
):
    count = qa_ref.shape[0] // block
    half = heads // 2
    starts = [pair_start(q_ref.shape[1], own) for own in (True, False)]
    causal = (
        lax.broadcasted_iota(jnp.int32, (block, block), 0)
        >= lax.broadcasted_iota(jnp.int32, (block, block), 1)
    ).astype(BF16)

    @pl.loop(0, count // 2)
    def _(c):
        for h in range(heads):
            ka_ref, va_ref, runs_ref = (
                (ka0_ref, va0_ref, runs0_ref) if h < half else (ka1_ref, va1_ref, runs1_ref)
            )
            i = h % half
            column = pl.ds(pl.multiple_of(starts[h // half] + i * DH, DH), DH)
            state = runs_ref[first // 2 + c, i]
            for odd in range(2):
                part = pl.ds(pl.multiple_of((2 * c + odd) * block, block), block)
                whole = pl.ds(pl.multiple_of((first + 2 * c + odd) * block, block), block)
                q = silu(q_ref[whole, column])
                k = ka_ref[whole, cols_of(i)]
                v = va_ref[whole, cols_of(i)]
                scores = dot(q, k, ((1,), (1,))).astype(BF16) * causal
                hi = state.astype(BF16)
                lo = (state - hi.astype(F32)).astype(BF16)
                left = jnp.concatenate([scores, q, q], axis=1)
                right = jnp.concatenate([v, hi, lo], axis=0)
                base_ref[part, cols_of(h)] = dot(left, right, ((1,), (0,)))
                qa_ref[part, cols_of(h)] = q
                if not odd:
                    state = state + dot(k, v, ((0,), (0,)))


def gate_kernel(block, own_ref, rest_ref, gate_hbm, gain_ref, out_ref, gate_in, sems):
    count = gate_in.shape[0] // block
    width = gate_in.shape[1]

    def copy(n):
        part = pl.ds(n * block, block)
        return pltpu.make_async_copy(gate_hbm.at[part], gate_in.at[part], sems.at[n])

    for n in range(count):
        copy(n).start()
    places = [pl.ds(pair_start(width, own), width // 2) for own in (True, False)]

    @pl.loop(0, count)
    def _(n):
        copy(n).wait()
        part = pl.ds(pl.multiple_of(n * block, block), block)
        for attn_ref, cols in zip((own_ref, rest_ref), places):
            sigmoid = 0.5 + 0.5 * jnp.tanh(gate_in[part, cols].astype(F32) * 0.5)
            out_ref[part, cols] = attn_ref[part] * (gain_ref[:, cols] * sigmoid)


def carry(pair, block, base_refs, qa_refs, state_ref, attn_ref, states, finish):
    half = state_ref.shape[0]
    for i in range(half):
        state = state_ref[i, :DH]
        hi = state.astype(BF16)
        states[i, :DH] = hi
        states[i, DH:] = (state - hi.astype(F32)).astype(BF16)
    first = 0
    for base_ref, qa_ref in zip(base_refs, qa_refs):

        @pl.loop(0, base_ref.shape[0] // block, unroll=True)
        def _(n):
            part = pl.ds(pl.multiple_of(n * block, block), block)
            whole = pl.ds(pl.multiple_of((first + n) * block, block), block)
            sums = None
            for i in range(half):
                wide = cols_of(pair * half + i)
                q = qa_ref[part, wide]
                attn = base_ref[part, wide] + dot(
                    jnp.concatenate([q, q], axis=1), states[i], ((1,), (0,))
                )
                attn_ref[whole, cols_of(i)] = attn
                sums = attn * attn if sums is None else sums + attn * attn
            finish(whole, sums)

        first += base_ref.shape[0] // block


def carry_own_kernel(
    block, base0_ref, base1_ref, qa0_ref, qa1_ref, keep_ref, attn_ref, sums_ref, states
):
    def finish(whole, sums):
        sums_ref[whole] = sums

    carry(0, block, (base0_ref, base1_ref), (qa0_ref, qa1_ref), keep_ref, attn_ref, states, finish)


def carry_rest_kernel(
    block, base0_ref, base1_ref, qa0_ref, qa1_ref, keep_ref, got_ref, sums_ref,
    attn_ref, mine_ref, states, squares,
):
    def finish(whole, sums):
        sums = sums + sums_ref[whole]
        hi = sums.astype(BF16)
        squares[whole, :DH] = hi
        squares[whole, DH:] = (sums - hi.astype(F32)).astype(BF16)

    carry(1, block, (base0_ref, base1_ref), (qa0_ref, qa1_ref), got_ref, attn_ref, states, finish)
    across = dot(jnp.ones((16, 2 * DH), BF16), squares[...], ((1,), (1,)))
    token_rows = squares.shape[0] // DH
    for c in range(token_rows):
        mine_ref[c : c + 1] = across[:1, cols_of(c)]
    core = lax.rem(lax.axis_index("seq"), 2)
    half, rows = keep_ref.shape[0], keep_ref.shape[1] - DH
    for i in range(half):
        for ref, h in ((keep_ref, core * half + i), (got_ref, (1 - core) * half + i)):
            mine_ref[pl.ds(pl.multiple_of(token_rows + h * rows, 8), rows)] = ref[i, DH:]


def pack_kernel(owners_ref, mine_ref, other_ref, send_ref):
    side = lax.rem(lax.axis_index("grp"), 2)
    rows = owners_ref.shape[1]
    width = mine_ref.shape[0]
    token_rows = width - 4 * rows
    own, other = owners_ref[0] - side, owners_ref[1] - side
    both = mine_ref[:token_rows] + other_ref[:token_rows]
    for place, g in enumerate(lines(2 * send_ref.shape[0])[0]):
        send_ref[place, :token_rows] = both
        for at in range(token_rows, width, rows):
            part = slice(at, at + rows)
            send_ref[place, part] = jnp.where(
                own == g, mine_ref[part], jnp.where(other == g, other_ref[part], 0.0)
            )


def norm_kernel(
    heads, features, block, got_ref, gated_ref, out_hbm, state_hbm, out, scales, final, sems, state_sem
):
    total = got_ref[0]
    for place in range(1, got_ref.shape[0]):
        total = total + got_ref[place]
    rows = final.shape[1]
    tokens = out.shape[0]
    token_rows = tokens // DH
    scales[...] = jnp.zeros_like(scales)
    scales[:token_rows] = lax.rsqrt(total[:token_rows] / features + 1e-6)
    columns = jnp.transpose(scales[...])
    for h in range(heads):
        at = token_rows + h * rows
        final[h] = total[at : at + rows]
    copies = [pltpu.make_async_copy(final, state_hbm, state_sem)]
    copies[0].start()
    for n in range(tokens // block):
        for c in range(n * block // DH, (n + 1) * block // DH):
            part = slice(c * DH, (c + 1) * DH)
            out[part] = (gated_ref[part] * columns[:, c : c + 1]).astype(BF16)
        part = pl.ds(n * block, block)
        copies.append(pltpu.make_async_copy(out.at[part], out_hbm.at[part], sems.at[n]))
        copies[-1].start()
    for copy in copies:
        copy.wait()


def body(query_in, key_in, value_in, gate_in, norm_gain, head_owner):
    tokens, width = query_in.shape
    heads = width // DH
    half = heads // 2
    shards = lax.axis_size("seq")
    groups = lax.axis_size("grp")
    chips = 4
    block = min(256, tokens)
    count = tokens // block
    chunk = 2 * block
    rows = DH // shards
    token_rows = tokens // DH
    wide = pltpu.VMEM((tokens, width), BF16)
    pair_state = pltpu.VMEM((half, DH, DH), F32)
    dma = lambda *shape: pltpu.SemaphoreType.DMA(shape)
    limit = params(24)

    half_wide = pltpu.VMEM((tokens, half * DH), BF16)
    runs = pltpu.VMEM((tokens // chunk, half, DH, DH), F32)
    k_in, v_in, ka1, va1, give, runs1 = pl.pallas_call(
        functools.partial(give_kernel, chunk),
        in_specs=[HBM] * 2,
        out_specs=[VMEM] * 6,
        out_shape=[wide] * 2 + [half_wide] * 2 + [pair_state, runs],
        scratch_shapes=[dma(2, tokens // chunk), dma(2)],
        compiler_params=limit,
        cost_estimate=cost(tokens * width * DH, 6 * tokens * width),
        name="give",
    )(in_hbm(key_in), in_hbm(value_in))

    def swap(x, bit):
        return lax.ppermute(x, "seq", [(i, i ^ bit) for i in range(shards)])

    def on_x(x, k):
        place = lambda i: i - i % (2 * chips) + (i + 2 * k) % (2 * chips)
        return lax.ppermute(x, "seq", [(i, place(i)) for i in range(shards)])

    def inside(first, blocks, q, acts):
        part = blocks * block
        return pl.pallas_call(
            functools.partial(inside_kernel, first, heads, block),
            in_specs=[VMEM] * 7,
            out_specs=[VMEM] * 2,
            out_shape=[
                pltpu.VMEM((part, width), F32),
                pltpu.VMEM((part, width), BF16),
            ],
            compiler_params=limit,
            cost_estimate=cost(2 * part * width * (2 * block + 3 * DH), 12 * part * width),
            name="inside%d" % first,
        )(q, *acts)

    cut = 6 * count // 8
    other = swap(give, 1)
    k_in, _ = lax.optimization_barrier((k_in, give))
    ka0, va0, mine, runs0, query, owners = pl.pallas_call(
        functools.partial(mine_kernel, chunk),
        in_specs=[VMEM, VMEM, HBM, HBM],
        out_specs=[VMEM] * 6,
        out_shape=[half_wide] * 2
        + [pair_state, runs, wide, pltpu.VMEM((2, rows, DH), jnp.int32)],
        scratch_shapes=[pltpu.SMEM(head_owner.shape, jnp.int32), dma(2)],
        compiler_params=limit,
        cost_estimate=cost(tokens * width * DH, 3 * tokens * width),
        name="mine",
    )(k_in, v_in, in_hbm(query_in), in_hbm(head_owner))
    other, mine = lax.optimization_barrier((other, mine))
    pair = pl.pallas_call(
        pair_kernel, in_specs=[VMEM] * 2, out_specs=VMEM, out_shape=pair_state,
        compiler_params=limit, name="pair",
    )(mine, other)
    around = [on_x(pair, k) for k in HOPS]
    acts = lax.optimization_barrier((ka0, va0, runs0, ka1, va1, runs1, pair))[:6]
    base0, qa0 = inside(0, cut, query, acts)
    base0, *around = lax.optimization_barrier((base0, *around))
    before_x, all_x = pl.pallas_call(
        functools.partial(along_x_kernel, chips),
        in_specs=[VMEM] * chips, out_specs=[VMEM] * 2, out_shape=[pair_state] * 2,
        compiler_params=limit, name="along_x",
    )(pair, *around)
    over = swap(all_x, 2 * chips)
    acts = lax.optimization_barrier((*acts, all_x))[:6]
    base1, qa1 = inside(cut, count - cut, query, acts)
    base1, over = lax.optimization_barrier((base1, over))
    keep, send_core = pl.pallas_call(
        functools.partial(along_y_kernel, chips),
        in_specs=[VMEM] * 5, out_specs=[VMEM] * 2,
        out_shape=[pltpu.VMEM((half, DH + rows, DH), F32)] * 2,
        compiler_params=limit, name="along_y",
    )(before_x, all_x, over, mine, other)
    got_core = swap(send_core, 1)
    payload = token_rows + heads * rows
    half_attn = pltpu.VMEM((tokens, half * DH), F32)
    states = pltpu.VMEM((half, 2 * DH, DH), BF16)
    attn_own, sums = pl.pallas_call(
        functools.partial(carry_own_kernel, block),
        in_specs=[VMEM] * 5,
        out_specs=[VMEM] * 2,
        out_shape=[half_attn, pltpu.VMEM((tokens, DH), F32)],
        scratch_shapes=[states],
        compiler_params=limit,
        cost_estimate=cost(2 * tokens * width * DH, 5 * tokens * width),
        name="carry_own",
    )(base0, base1, qa0, qa1, keep)
    sums, got_core = lax.optimization_barrier((sums, got_core))
    attn_rest, own = pl.pallas_call(
        functools.partial(carry_rest_kernel, block),
        in_specs=[VMEM] * 7,
        out_specs=[VMEM] * 2,
        out_shape=[half_attn, pltpu.VMEM((payload, DH), F32)],
        scratch_shapes=[states, pltpu.VMEM((tokens, 2 * DH), BF16)],
        compiler_params=limit,
        cost_estimate=cost(2 * tokens * width * DH, 5 * tokens * width),
        name="carry_rest",
    )(base0, base1, qa0, qa1, keep, got_core, sums)

    beside = lax.ppermute(own, "grp", [(g, g ^ 1) for g in range(groups)])
    gated = pl.pallas_call(
        functools.partial(gate_kernel, block),
        in_specs=[VMEM, VMEM, HBM, VMEM],
        out_specs=VMEM,
        out_shape=pltpu.VMEM((tokens, width), F32),
        scratch_shapes=[pltpu.VMEM((tokens, width), BF16), dma(count)],
        compiler_params=limit,
        cost_estimate=cost(4 * tokens * width, 10 * tokens * width),
        name="gate",
    )(attn_own, attn_rest, in_hbm(gate_in), norm_gain.reshape(1, width))
    gated, beside = lax.optimization_barrier((gated, beside))
    send = pl.pallas_call(
        pack_kernel,
        in_specs=[VMEM] * 3,
        out_specs=VMEM,
        out_shape=pltpu.VMEM((groups // 2, payload, DH), F32),
        compiler_params=limit,
        name="pack",
    )(owners, own, beside)

    got = lax.all_to_all(
        send, "grp", 0, 0, tiled=True, axis_index_groups=lines(groups)
    )

    attn_out, decode_state = pl.pallas_call(
        functools.partial(norm_kernel, heads, float(width * groups), block),
        in_specs=[VMEM, VMEM],
        out_specs=[HBM, HBM],
        out_shape=[
            jax.ShapeDtypeStruct((tokens, width), BF16),
            jax.ShapeDtypeStruct((heads, rows, DH), F32),
        ],
        scratch_shapes=[
            pltpu.VMEM((tokens, width), BF16),
            pltpu.VMEM((DH, DH), F32),
            pltpu.VMEM((heads, rows, DH), F32),
            dma(count),
            pltpu.SemaphoreType.DMA,
        ],
        compiler_params=limit,
        cost_estimate=cost(2 * tokens * width, 6 * tokens * width),
        name="norm",
    )(got, gated)
    return attn_out, decode_state


def solution(mesh):
    return jax.shard_map(
        body,
        mesh=mesh,
        in_specs=(
            P("seq", "grp"),
            P("seq", "grp"),
            P("seq", "grp"),
            P("seq", "grp"),
            P("grp"),
            P(),
        ),
        out_specs=(P("seq", "grp"), P("grp", "seq", None)),
        check_vma=False,
    )
```

```python
import functools

import jax
import jax.numpy as jnp
from jax import lax
from jax.experimental import pallas as pl
from jax.experimental.pallas import tpu as pltpu
from jax.sharding import PartitionSpec as P

DH = 128
HOPS = (2, 3, 1)
F32 = jnp.float32
BF16 = jnp.bfloat16
MIB = 1 << 20
VMEM = pl.BlockSpec(memory_space=pltpu.VMEM)
HBM = pl.BlockSpec(memory_space=pltpu.HBM)


def lines(groups):
    count = groups // 2
    order = [6, 5, 4, 7, 3, 2, 1, 0] if count == 8 else list(range(count))[::-1]
    return [[2 * at + side for at in order] for side in range(2)]


def dot(a, b, dims):
    return lax.dot_general(a, b, (dims, ((), ())), preferred_element_type=F32)


def silu(x):
    half = x.astype(F32) * 0.5
    return (half + half * jnp.tanh(half)).astype(BF16)


def params(mib):
    return pltpu.CompilerParams(vmem_limit_bytes=mib * MIB)


def cost(flops, nbytes, trans=0):
    return pl.CostEstimate(flops=flops, bytes_accessed=nbytes, transcendentals=trans)


def in_hbm(x):
    return pltpu.with_memory_space_constraint(x, pltpu.HBM)


def cols_of(h):
    return slice(h * DH, (h + 1) * DH)


def pair_start(width, own):
    core = lax.rem(lax.axis_index("seq"), 2)
    return pl.multiple_of((core if own else 1 - core) * (width // 2), width // 2)


def add_states(first, c, part, k_in, v_in, ka_ref, va_ref, state_ref, runs_ref):
    runs_ref[c] = state_ref[...]
    for i in range(state_ref.shape[0]):
        wide = pl.ds(pl.multiple_of(first + i * DH, DH), DH)
        k = silu(k_in[part, wide])
        v = silu(v_in[part, wide])
        ka_ref[part, cols_of(i)] = k
        va_ref[part, cols_of(i)] = v
        state_ref[i] += dot(k, v, ((0,), (0,)))


def give_kernel(
    chunk, k_hbm, v_hbm, k_in, v_in, ka_ref, va_ref, give_ref, runs_ref, sems, late
):
    tokens, width = k_in.shape
    count = tokens // chunk
    first = pair_start(width, False)

    def pair(c):
        place = (pl.ds(c * chunk, chunk), pl.ds(first, width // 2))
        return [
            pltpu.make_async_copy(k_hbm.at[place], k_in.at[place], sems.at[0, c]),
            pltpu.make_async_copy(v_hbm.at[place], v_in.at[place], sems.at[1, c]),
        ]

    own = (slice(None), pl.ds(pair_start(width, True), width // 2))
    later = [
        pltpu.make_async_copy(k_hbm.at[own], k_in.at[own], late.at[0]),
        pltpu.make_async_copy(v_hbm.at[own], v_in.at[own], late.at[1]),
    ]
    for c in range(count):
        for copy in pair(c):
            copy.start()
    for copy in later:
        copy.start()
    give_ref[...] = jnp.zeros_like(give_ref)

    @pl.loop(0, count)
    def _(c):
        for copy in pair(c):
            copy.wait()
        part = pl.ds(pl.multiple_of(c * chunk, chunk), chunk)
        add_states(first, c, part, k_in, v_in, ka_ref, va_ref, give_ref, runs_ref)

    for copy in later:
        copy.wait()


def mine_kernel(
    chunk, k_in, v_in, q_hbm, owner_hbm, ka_ref, va_ref, mine_ref, runs_ref, q_ref, owners_ref, owner, sems
):
    copies = [
        pltpu.make_async_copy(q_hbm, q_ref, sems.at[0]),
        pltpu.make_async_copy(owner_hbm, owner, sems.at[1]),
    ]
    for copy in copies:
        copy.start()
    mine_ref[...] = jnp.zeros_like(mine_ref)
    first = pair_start(k_in.shape[1], True)

    @pl.loop(0, k_in.shape[0] // chunk)
    def _(c):
        part = pl.ds(pl.multiple_of(c * chunk, chunk), chunk)
        add_states(first, c, part, k_in, v_in, ka_ref, va_ref, mine_ref, runs_ref)

    for copy in copies:
        copy.wait()
    group = lax.axis_index("grp")
    for at, g in enumerate((group, group + 1 - 2 * lax.rem(group, 2))):
        owners_ref[at] = jnp.full(owners_ref.shape[1:], owner[g], jnp.int32)


def pair_kernel(mine_ref, other_ref, out_ref):
    out_ref[...] = mine_ref[...] + other_ref[...]


def along_x_kernel(chips, own_ref, *refs):
    got, (before_ref, all_ref) = refs[: chips - 1], refs[chips - 1 :]
    x = lax.rem(lax.div(lax.axis_index("seq"), 2), chips)
    total = own_ref[...]
    before = jnp.zeros_like(total)
    for back in range(1, chips):
        part = got[HOPS.index(back)][...]
        total = total + part
        before = before + jnp.where(x >= back, part, 0.0)
    before_ref[...] = before
    all_ref[...] = total


def along_y_kernel(chips, before_ref, all_ref, over_ref, mine_ref, other_ref, keep_ref, send_ref):
    at = lax.axis_index("seq")
    core = lax.rem(at, 2)
    y = lax.div(at, 2 * chips)
    before = before_ref[...] + jnp.where(y > 0, over_ref[...], 0.0)
    keep_ref[:, :DH] = before + jnp.where(core > 0, other_ref[...], 0.0)
    send_ref[:, :DH] = before + jnp.where(core > 0, 0.0, mine_ref[...])
    rows = keep_ref.shape[1] - DH
    partner = at + 1 - 2 * core
    for i in range(keep_ref.shape[0]):
        for ref, place in ((keep_ref, at), (send_ref, partner)):
            some = pl.ds(pl.multiple_of(place * rows, 8), rows)
            ref[i, DH:] = all_ref[i, some] + over_ref[i, some]


def inside_kernel(
    first, heads, block, q_ref, ka0_ref, va0_ref, runs0_ref, ka1_ref, va1_ref, runs1_ref,
    base_ref, qa_ref,
):
    count = qa_ref.shape[0] // block
    half = heads // 2
    starts = [pair_start(q_ref.shape[1], own) for own in (True, False)]
    causal = (
        lax.broadcasted_iota(jnp.int32, (block, block), 0)
        >= lax.broadcasted_iota(jnp.int32, (block, block), 1)
    ).astype(BF16)

    @pl.loop(0, count // 2)
    def _(c):
        for h in range(heads):
            ka_ref, va_ref, runs_ref = (
                (ka0_ref, va0_ref, runs0_ref) if h < half else (ka1_ref, va1_ref, runs1_ref)
            )
            i = h % half
            column = pl.ds(pl.multiple_of(starts[h // half] + i * DH, DH), DH)
            state = runs_ref[first // 2 + c, i]
            for odd in range(2):
                part = pl.ds(pl.multiple_of((2 * c + odd) * block, block), block)
                whole = pl.ds(pl.multiple_of((first + 2 * c + odd) * block, block), block)
                q = silu(q_ref[whole, column])
                k = ka_ref[whole, cols_of(i)]
                v = va_ref[whole, cols_of(i)]
                scores = dot(q, k, ((1,), (1,))).astype(BF16) * causal
                hi = state.astype(BF16)
                lo = (state - hi.astype(F32)).astype(BF16)
                left = jnp.concatenate([scores, q, q], axis=1)
                right = jnp.concatenate([v, hi, lo], axis=0)
                base_ref[part, cols_of(h)] = dot(left, right, ((1,), (0,)))
                qa_ref[part, cols_of(h)] = q
                if not odd:
                    state = state + dot(k, v, ((0,), (0,)))


def gate_kernel(block, own_ref, rest_ref, gate_hbm, gain_ref, out_ref, gate_in, sems):
    count = gate_in.shape[0] // block
    width = gate_in.shape[1]

    def copy(n):
        part = pl.ds(n * block, block)
        return pltpu.make_async_copy(gate_hbm.at[part], gate_in.at[part], sems.at[n])

    for n in range(count):
        copy(n).start()
    places = [pl.ds(pair_start(width, own), width // 2) for own in (True, False)]

    @pl.loop(0, count)
    def _(n):
        copy(n).wait()
        part = pl.ds(pl.multiple_of(n * block, block), block)
        for attn_ref, cols in zip((own_ref, rest_ref), places):
            sigmoid = 0.5 + 0.5 * jnp.tanh(gate_in[part, cols].astype(F32) * 0.5)
            out_ref[part, cols] = attn_ref[part] * (gain_ref[:, cols] * sigmoid)


def carry(pair, block, base_refs, qa_refs, state_ref, attn_ref, states, finish):
    half = state_ref.shape[0]
    for i in range(half):
        state = state_ref[i, :DH]
        hi = state.astype(BF16)
        states[i, :DH] = hi
        states[i, DH:] = (state - hi.astype(F32)).astype(BF16)
    first = 0
    for base_ref, qa_ref in zip(base_refs, qa_refs):

        @pl.loop(0, base_ref.shape[0] // block, unroll=True)
        def _(n):
            part = pl.ds(pl.multiple_of(n * block, block), block)
            whole = pl.ds(pl.multiple_of((first + n) * block, block), block)
            sums = None
            for i in range(half):
                wide = cols_of(pair * half + i)
                q = qa_ref[part, wide]
                attn = base_ref[part, wide] + dot(
                    jnp.concatenate([q, q], axis=1), states[i], ((1,), (0,))
                )
                attn_ref[whole, cols_of(i)] = attn
                sums = attn * attn if sums is None else sums + attn * attn
            finish(whole, sums)

        first += base_ref.shape[0] // block


def carry_own_kernel(
    block, base0_ref, base1_ref, qa0_ref, qa1_ref, keep_ref, attn_ref, sums_ref, states
):
    def finish(whole, sums):
        sums_ref[whole] = sums

    carry(0, block, (base0_ref, base1_ref), (qa0_ref, qa1_ref), keep_ref, attn_ref, states, finish)


def carry_rest_kernel(
    block, base0_ref, base1_ref, qa0_ref, qa1_ref, keep_ref, got_ref, sums_ref,
    attn_ref, mine_ref, states, squares,
):
    def finish(whole, sums):
        sums = sums + sums_ref[whole]
        hi = sums.astype(BF16)
        squares[whole, :DH] = hi
        squares[whole, DH:] = (sums - hi.astype(F32)).astype(BF16)

    carry(1, block, (base0_ref, base1_ref), (qa0_ref, qa1_ref), got_ref, attn_ref, states, finish)
    across = dot(jnp.ones((16, 2 * DH), BF16), squares[...], ((1,), (1,)))
    token_rows = squares.shape[0] // DH
    for c in range(token_rows):
        mine_ref[c : c + 1] = across[:1, cols_of(c)]
    core = lax.rem(lax.axis_index("seq"), 2)
    half, rows = keep_ref.shape[0], keep_ref.shape[1] - DH
    for i in range(half):
        for ref, h in ((keep_ref, core * half + i), (got_ref, (1 - core) * half + i)):
            mine_ref[pl.ds(pl.multiple_of(token_rows + h * rows, 8), rows)] = ref[i, DH:]


def pack_kernel(owners_ref, mine_ref, other_ref, send_ref):
    side = lax.rem(lax.axis_index("grp"), 2)
    rows = owners_ref.shape[1]
    width = mine_ref.shape[0]
    token_rows = width - 4 * rows
    own, other = owners_ref[0] - side, owners_ref[1] - side
    both = mine_ref[:token_rows] + other_ref[:token_rows]
    for place, g in enumerate(lines(2 * send_ref.shape[0])[0]):
        send_ref[place, :token_rows] = both
        for at in range(token_rows, width, rows):
            part = slice(at, at + rows)
            send_ref[place, part] = jnp.where(
                own == g, mine_ref[part], jnp.where(other == g, other_ref[part], 0.0)
            )


def norm_kernel(
    heads, features, block, got_ref, gated_ref, out_hbm, state_hbm, out, scales, final, sems, state_sem
):
    rows = final.shape[1]
    tokens = out.shape[0]
    token_rows = tokens // DH
    total = got_ref[0, :token_rows]
    for place in range(1, got_ref.shape[0]):
        total = total + got_ref[place, :token_rows]
    scales[...] = jnp.zeros_like(scales)
    scales[:token_rows] = lax.rsqrt(total / features + 1e-6)
    columns = jnp.transpose(scales[...])
    copies = []
    for n in range(tokens // block):
        for c in range(n * block // DH, (n + 1) * block // DH):
            part = slice(c * DH, (c + 1) * DH)
            out[part] = (gated_ref[part] * columns[:, c : c + 1]).astype(BF16)
        part = pl.ds(n * block, block)
        copies.append(pltpu.make_async_copy(out.at[part], out_hbm.at[part], sems.at[n]))
        copies[-1].start()
        if n == 0:
            for h in range(heads):
                part = slice(token_rows + h * rows, token_rows + (h + 1) * rows)
                rest = got_ref[0, part]
                for place in range(1, got_ref.shape[0]):
                    rest = rest + got_ref[place, part]
                final[h] = rest
            copies.append(pltpu.make_async_copy(final, state_hbm, state_sem))
            copies[-1].start()
    for copy in copies:
        copy.wait()


def body(query_in, key_in, value_in, gate_in, norm_gain, head_owner):
    tokens, width = query_in.shape
    heads = width // DH
    half = heads // 2
    shards = lax.axis_size("seq")
    groups = lax.axis_size("grp")
    chips = 4
    block = min(256, tokens)
    count = tokens // block
    chunk = 2 * block
    rows = DH // shards
    token_rows = tokens // DH
    wide = pltpu.VMEM((tokens, width), BF16)
    pair_state = pltpu.VMEM((half, DH, DH), F32)
    dma = lambda *shape: pltpu.SemaphoreType.DMA(shape)
    limit = params(24)

    half_wide = pltpu.VMEM((tokens, half * DH), BF16)
    runs = pltpu.VMEM((tokens // chunk, half, DH, DH), F32)
    k_in, v_in, ka1, va1, give, runs1 = pl.pallas_call(
        functools.partial(give_kernel, chunk),
        in_specs=[HBM] * 2,
        out_specs=[VMEM] * 6,
        out_shape=[wide] * 2 + [half_wide] * 2 + [pair_state, runs],
        scratch_shapes=[dma(2, tokens // chunk), dma(2)],
        compiler_params=limit,
        cost_estimate=cost(tokens * width * DH, 6 * tokens * width),
        name="give",
    )(in_hbm(key_in), in_hbm(value_in))

    def swap(x, bit):
        return lax.ppermute(x, "seq", [(i, i ^ bit) for i in range(shards)])

    def on_x(x, k):
        place = lambda i: i - i % (2 * chips) + (i + 2 * k) % (2 * chips)
        return lax.ppermute(x, "seq", [(i, place(i)) for i in range(shards)])

    def inside(first, blocks, q, acts):
        part = blocks * block
        return pl.pallas_call(
            functools.partial(inside_kernel, first, heads, block),
            in_specs=[VMEM] * 7,
            out_specs=[VMEM] * 2,
            out_shape=[
                pltpu.VMEM((part, width), F32),
                pltpu.VMEM((part, width), BF16),
            ],
            compiler_params=limit,
            cost_estimate=cost(2 * part * width * (2 * block + 3 * DH), 12 * part * width),
            name="inside%d" % first,
        )(q, *acts)

    cut = 6 * count // 8
    other = swap(give, 1)
    k_in, _ = lax.optimization_barrier((k_in, give))
    ka0, va0, mine, runs0, query, owners = pl.pallas_call(
        functools.partial(mine_kernel, chunk),
        in_specs=[VMEM, VMEM, HBM, HBM],
        out_specs=[VMEM] * 6,
        out_shape=[half_wide] * 2
        + [pair_state, runs, wide, pltpu.VMEM((2, rows, DH), jnp.int32)],
        scratch_shapes=[pltpu.SMEM(head_owner.shape, jnp.int32), dma(2)],
        compiler_params=limit,
        cost_estimate=cost(tokens * width * DH, 3 * tokens * width),
        name="mine",
    )(k_in, v_in, in_hbm(query_in), in_hbm(head_owner))
    other, mine = lax.optimization_barrier((other, mine))
    pair = pl.pallas_call(
        pair_kernel, in_specs=[VMEM] * 2, out_specs=VMEM, out_shape=pair_state,
        compiler_params=limit, name="pair",
    )(mine, other)
    around = [on_x(pair, k) for k in HOPS]
    acts = lax.optimization_barrier((ka0, va0, runs0, ka1, va1, runs1, pair))[:6]
    base0, qa0 = inside(0, cut, query, acts)
    base0, *around = lax.optimization_barrier((base0, *around))
    before_x, all_x = pl.pallas_call(
        functools.partial(along_x_kernel, chips),
        in_specs=[VMEM] * chips, out_specs=[VMEM] * 2, out_shape=[pair_state] * 2,
        compiler_params=limit, name="along_x",
    )(pair, *around)
    over = swap(all_x, 2 * chips)
    acts = lax.optimization_barrier((*acts, all_x))[:6]
    base1, qa1 = inside(cut, count - cut, query, acts)
    base1, over = lax.optimization_barrier((base1, over))
    keep, send_core = pl.pallas_call(
        functools.partial(along_y_kernel, chips),
        in_specs=[VMEM] * 5, out_specs=[VMEM] * 2,
        out_shape=[pltpu.VMEM((half, DH + rows, DH), F32)] * 2,
        compiler_params=limit, name="along_y",
    )(before_x, all_x, over, mine, other)
    got_core = swap(send_core, 1)
    payload = token_rows + heads * rows
    half_attn = pltpu.VMEM((tokens, half * DH), F32)
    states = pltpu.VMEM((half, 2 * DH, DH), BF16)
    attn_own, sums = pl.pallas_call(
        functools.partial(carry_own_kernel, block),
        in_specs=[VMEM] * 5,
        out_specs=[VMEM] * 2,
        out_shape=[half_attn, pltpu.VMEM((tokens, DH), F32)],
        scratch_shapes=[states],
        compiler_params=limit,
        cost_estimate=cost(2 * tokens * width * DH, 5 * tokens * width),
        name="carry_own",
    )(base0, base1, qa0, qa1, keep)
    sums, got_core = lax.optimization_barrier((sums, got_core))
    attn_rest, own = pl.pallas_call(
        functools.partial(carry_rest_kernel, block),
        in_specs=[VMEM] * 7,
        out_specs=[VMEM] * 2,
        out_shape=[half_attn, pltpu.VMEM((payload, DH), F32)],
        scratch_shapes=[states, pltpu.VMEM((tokens, 2 * DH), BF16)],
        compiler_params=limit,
        cost_estimate=cost(2 * tokens * width * DH, 5 * tokens * width),
        name="carry_rest",
    )(base0, base1, qa0, qa1, keep, got_core, sums)

    beside = lax.ppermute(own, "grp", [(g, g ^ 1) for g in range(groups)])
    gated = pl.pallas_call(
        functools.partial(gate_kernel, block),
        in_specs=[VMEM, VMEM, HBM, VMEM],
        out_specs=VMEM,
        out_shape=pltpu.VMEM((tokens, width), F32),
        scratch_shapes=[pltpu.VMEM((tokens, width), BF16), dma(count)],
        compiler_params=limit,
        cost_estimate=cost(4 * tokens * width, 10 * tokens * width),
        name="gate",
    )(attn_own, attn_rest, in_hbm(gate_in), norm_gain.reshape(1, width))
    gated, beside = lax.optimization_barrier((gated, beside))
    send = pl.pallas_call(
        pack_kernel,
        in_specs=[VMEM] * 3,
        out_specs=VMEM,
        out_shape=pltpu.VMEM((groups // 2, payload, DH), F32),
        compiler_params=limit,
        name="pack",
    )(owners, own, beside)

    got = lax.all_to_all(
        send, "grp", 0, 0, tiled=True, axis_index_groups=lines(groups)
    )

    attn_out, decode_state = pl.pallas_call(
        functools.partial(norm_kernel, heads, float(width * groups), block),
        in_specs=[VMEM, VMEM],
        out_specs=[HBM, HBM],
        out_shape=[
            jax.ShapeDtypeStruct((tokens, width), BF16),
            jax.ShapeDtypeStruct((heads, rows, DH), F32),
        ],
        scratch_shapes=[
            pltpu.VMEM((tokens, width), BF16),
            pltpu.VMEM((DH, DH), F32),
            pltpu.VMEM((heads, rows, DH), F32),
            dma(count),
            pltpu.SemaphoreType.DMA,
        ],
        compiler_params=limit,
        cost_estimate=cost(2 * tokens * width, 6 * tokens * width),
        name="norm",
    )(got, gated)
    return attn_out, decode_state


def solution(mesh):
    return jax.shard_map(
        body,
        mesh=mesh,
        in_specs=(
            P("seq", "grp"),
            P("seq", "grp"),
            P("seq", "grp"),
            P("seq", "grp"),
            P("grp"),
            P(),
        ),
        out_specs=(P("seq", "grp"), P("grp", "seq", None)),
        check_vma=False,
    )
```
